32 devices in a mesh: groups: 2 (over x), slab: 16 (over z, y, core).
Axes of the slice: x: 2, y: 2, z: 4, core: 2. Of those that a mesh axis runs over, the one named last changes fastest.
Arguments:
- volume: bfloat16 [64, 48, 48, 128], P(('groups', 'slab')), parts along dimension 0, may hold values from -6 to 6
- kernel: bfloat16 [3, 3, 3, 128, 128], replicated, may hold values from -0.109375 to 0.109375
- grad_out: bfloat16 [64, 48, 48, 128], P(('groups', 'slab')), parts along dimension 0, may hold values from -6 to 6
Outputs:
- activation: bfloat16 [64, 48, 48, 128], P(('groups', 'slab')), parts along dimension 0
- input_grad: bfloat16 [64, 48, 48, 128], P(('groups', 'slab')), parts along dimension 0
- weight_grad: float32 [6, 3, 3, 128, 128], P('groups'), parts along dimension 0
The draws below stay inside these ranges and needn't reach their ends.
There are 2 independent parts, one for each index of `groups`. The reference program is written for one: setup_inputs(seed, part) draws one part's arguments, and reference() takes and returns one part's arrays. A program takes and returns all parts, laid end to end along the dimension named above; an argument that names none is the same for every part. Nothing has to cross between parts.
All inputs are finite; a program needn't handle non-finite values.
Results may differ from the reference program's by a relative error of at most 0.001.
Values may be sent and summed in bfloat16 or wider, within the bound.
A program may use at most 64 MiB of HBM per device.

```python
import jax
import jax.numpy as jnp
from jax import lax

C = 128
HEIGHT = 48
BREADTH = 48
DEPTH = 32


def shard_levels(rng, dims, cuts, smallest, top_value):
    def one(dim, shards_of):
        steps = jax.random.uniform(jax.random.fold_in(jax.random.fold_in(rng, 6), dim), (shards_of,), jnp.float32, smallest / len(cuts), top_value / len(cuts))
        return jnp.repeat(jnp.exp(steps), dims[dim] // shards_of).reshape((-1,) + (1,) * (len(dims) - dim - 1))

    level = one(*cuts[0])
    for cut in cuts[1:]:
        level = level * one(*cut)
    return level


def bell_draw(key, shape, width, reach, pieces=(), kind=jnp.bfloat16):
    result = jax.random.normal(key, shape, jnp.float32) * width
    if len(pieces) > 0:
        result = shard_levels(key, shape, pieces, -0.22, 0.18) * result
    return jnp.clip(result, min=-reach, max=reach).astype(kind)


def setup_inputs(seed: int = 0, part: int = 0) -> dict:
    arg_keys = jax.random.split(jax.random.key(seed), 4)
    part_splits = jax.random.split(jax.random.fold_in(arg_keys[3], part), 4)
    volume = bell_draw(part_splits[0], (DEPTH, HEIGHT, BREADTH, C), 1.0, 6.0, ((0, 16),))
    kernel = bell_draw(arg_keys[1], (3, 3, 3, C, C), (27 * C) ** -0.5, 0.109375)
    grad_out = bell_draw(part_splits[2], (DEPTH, HEIGHT, BREADTH, C), 1.0, 6.0, ((0, 16),))
    return {"volume": volume, "kernel": kernel, "grad_out": grad_out}


def plane_conv(padded, kernel, plane):
    height = padded.shape[1] - 2
    breadth = padded.shape[2] - 2
    channels = padded.shape[3]
    window = lax.dynamic_slice_in_dim(padded, plane, 3, 0)
    total = jnp.zeros((height * breadth, kernel.shape[4]), jnp.float32)
    for depth_off in range(3):
        for row_off in range(3):
            for col_off in range(3):
                cells = window[depth_off, row_off:row_off + height, col_off:col_off + breadth, :]
                total = total + jnp.dot(cells.reshape(height * breadth, channels), kernel[depth_off, row_off, col_off], preferred_element_type=jnp.float32)
    return total.reshape(height, breadth, kernel.shape[4]).astype(jnp.bfloat16)

def full_conv(padded, kernel, depth):
    planes = jnp.arange(depth, dtype=jnp.int32)
    return lax.map(lambda plane: plane_conv(padded, kernel, plane), planes)

def reference(volume, kernel, grad_out):
    depth, height, breadth, channels = volume.shape
    padded = jnp.pad(volume, ((1, 1), (1, 1), (1, 1), (0, 0)))
    activation = full_conv(padded, kernel, depth)
    grad_padded = jnp.pad(grad_out, ((1, 1), (1, 1), (1, 1), (0, 0)))
    flipped = jnp.swapaxes(kernel[::-1, ::-1, ::-1], 3, 4)
    input_grad = full_conv(grad_padded, flipped, depth)

    def accumulate(carry, plane):
        window = lax.dynamic_slice_in_dim(padded, plane, 3, 0)
        grads = lax.dynamic_slice_in_dim(grad_out, plane, 1, 0)[0].reshape(height * breadth, channels)
        rows = []
        for depth_off in range(3):
            for row_off in range(3):
                for col_off in range(3):
                    cells = window[depth_off, row_off:row_off + height, col_off:col_off + breadth, :]
                    cells = cells.reshape(height * breadth, channels)
                    rows.append(jnp.dot(cells.T, grads, preferred_element_type=jnp.float32))
        update = jnp.stack(rows).reshape(3, 3, 3, channels, channels)
        return (carry + update, None)
    start = jnp.zeros((3, 3, 3, channels, channels), jnp.float32)
    summed, _ = lax.scan(accumulate, start, jnp.arange(depth, dtype=jnp.int32))
    cells_all = depth * height * breadth
    weight_grad = summed / jnp.sqrt(jnp.float32(cells_all))
    return (activation, input_grad, weight_grad)
```

```python
import functools

import jax
import jax.numpy as jnp
import numpy as np
from jax import lax
from jax.experimental import pallas as pl
from jax.experimental.pallas import tpu as pltpu
from jax.sharding import PartitionSpec as P

MESH = pl.DeviceIdType.MESH
F32 = jnp.float32
BF16 = jnp.bfloat16


def layer_kernel(
    n, line, cols, height, breadth, ch, tile, factor,
    vol, ker, grd,
    act_out, ing_out, dw_out,
    vp, gp, wf, wb, xt, gs, acc, fin, r_sib, r_lo, r_hi, r_y, act, ing,
    s_in, s_w, s_hs, s_hr, s_sib, r_sibs, s_line, r_los, r_his, s_y, r_ys,
    s_up, s_dn, s_fs, r_fin, r_fsib, s_out,
):
    cells = height * breadth
    half = ch // 2
    taps = 9
    me = lax.axis_index("slab")
    core = lax.rem(me, 2)
    chip = me // 2
    z = chip // cols
    y = lax.rem(chip, cols)
    sib = me + 1 - 2 * core
    zlo = me - 2 * cols
    zhi = me + 2 * cols
    has_lo, has_hi = z > 0, z < line - 1
    has_before, has_after = me > 0, me < n - 1

    def peer(k):
        return (z * cols + lax.rem(y + k, cols)) * 2 + core

    inner = pl.ds(breadth, cells)
    loads = []
    for p in range(2):
        loads.append(pltpu.make_async_copy(vol.at[p], vp.at[p + 1, inner], s_in.at[p]))
    for p in range(2):
        loads.append(pltpu.make_async_copy(grd.at[p], gp.at[p + 1, inner], s_in.at[p + 2]))
    for copy in loads:
        copy.start()
    wloads = []
    for a in range(3):
        for d in range(2):
            p = a + d
            wloads.append(pltpu.make_async_copy(
                ker.at[a], wf.at[:, :, pl.ds(p * ch, ch), pl.ds(d * ch, ch)], s_w.at[0, a, d]))
            p = d + 2 - a
            wloads.append(pltpu.make_async_copy(
                ker.at[a], wb.at[:, :, pl.ds(d * ch, ch), pl.ds(p * ch, ch)], s_w.at[1, a, d]))
    for copy in wloads:
        copy.start()

    barrier = pltpu.get_barrier_semaphore()

    def greet(dev):
        pl.semaphore_signal(barrier, inc=1, device_id={"slab": dev}, device_id_type=MESH)

    for k in range(1, cols):
        greet(peer(k))
    for cond, dev in ((has_before, me - 1), (has_after, me + 1), (has_lo, zlo), (has_hi, zhi)):
        @pl.when(cond)
        def _(dev=dev):
            greet(dev)
    partners = cols - 1
    for cond in (has_before, has_after, has_lo, has_hi):
        partners = partners + cond.astype(jnp.int32)
    pl.semaphore_wait(barrier, partners)

    def remote(src, dst, ssem, rsem, dev):
        return pltpu.make_async_remote_copy(
            src_ref=src, dst_ref=dst, send_sem=ssem, recv_sem=rsem,
            device_id={"slab": dev}, device_id_type=MESH)

    def halo(which, src, dst, up):
        if up:
            return remote(src.at[1], dst.at[0, inner], s_hs.at[which, 0], s_hr.at[which, 0], me + 1)
        return remote(src.at[0], dst.at[3, inner], s_hs.at[which, 1], s_hr.at[which, 1], me - 1)

    for which, src, dst in ((0, vol, vp), (1, grd, gp)):
        @pl.when(has_after)
        def _(which=which, src=src, dst=dst):
            halo(which, src, dst, True).start()

        @pl.when(has_before)
        def _(which=which, src=src, dst=dst):
            halo(which, src, dst, False).start()

    edge = jnp.zeros((breadth, ch), BF16)
    for ref in (vp, gp):
        for p in range(4):
            ref[p, pl.ds(0, breadth), :] = edge
            ref[p, pl.ds(breadth + cells, breadth), :] = edge
    edge2 = jnp.zeros((breadth, 2 * ch), BF16)
    for c in range(3):
        gs[c, pl.ds(0, breadth), :] = edge2
        gs[c, pl.ds(breadth + cells, breadth), :] = edge2
    blank = jnp.zeros((3, 3, ch, ch), BF16)
    wf[:, :, pl.ds(0, ch), pl.ds(ch, ch)] = blank
    wf[:, :, pl.ds(3 * ch, ch), pl.ds(0, ch)] = blank
    wb[:, :, pl.ds(0, ch), pl.ds(3 * ch, ch)] = blank
    wb[:, :, pl.ds(ch, ch), pl.ds(0, ch)] = blank
    for cond, p in ((me == 0, 0), (me == n - 1, 3)):
        @pl.when(cond)
        def _(p=p):
            vp[p, inner, :] = jnp.zeros((cells, ch), BF16)
            gp[p, inner, :] = jnp.zeros((cells, ch), BF16)

    rows = tile * breadth
    tiles = height // tile
    column = lax.rem(lax.broadcasted_iota(jnp.int32, (rows, 2 * ch), 0), breadth)

    def before_of(v):
        return jnp.where(column == 0, 0.0, pltpu.roll(v, 1, 0))

    def after_of(v):
        return jnp.where(column == breadth - 1, 0.0, pltpu.roll(v, rows - 1, 0))

    for copy in loads:
        copy.wait()

    def shift_tile(k, carry):
        at = pl.ds(pl.multiple_of(breadth + k * rows, 16), rows)
        both = jnp.concatenate([gp[1, at, :], gp[2, at, :]], axis=1)
        wide = both.astype(F32)
        gs[0, at, :] = after_of(wide).astype(BF16)
        gs[1, at, :] = both
        gs[2, at, :] = before_of(wide).astype(BF16)
        return carry

    lax.fori_loop(0, tiles, shift_tile, 0)

    def transpose_planes(lo, hi, at_row):
        def one(j, carry):
            at = pl.ds(pl.multiple_of(breadth + j * ch, 16), ch)
            to = pl.ds(pl.multiple_of(j * ch, ch), ch)
            xt[pl.ds(at_row, ch), to] = vp[lo, at, :].T
            xt[pl.ds(at_row + ch, ch), to] = vp[hi, at, :].T
            return carry
        lax.fori_loop(0, cells // ch, one, 0)

    def products(t, at_row):
        b, c = t // 3, lax.rem(t, 3)
        at = pl.ds(pl.multiple_of((2 - b) * breadth, 16), cells)
        return jnp.dot(xt[pl.ds(at_row, 2 * ch), :], gs[c, at, :], preferred_element_type=F32)

    transpose_planes(1, 2, 0)

    def own_part(t, carry):
        full = products(t, 0)
        acc[0, t] = full[:ch, ch:]
        acc[1, t] = full[:ch, :ch] + full[ch:, ch:]
        acc[2, t] = full[ch:, :ch]
        return carry

    lax.fori_loop(0, taps, own_part, 0)

    def halo_wait(which, src, dst):
        @pl.when(has_before)
        def _():
            halo(which, src, dst, True).wait_recv()

        @pl.when(has_after)
        def _():
            halo(which, src, dst, False).wait_recv()

    halo_wait(0, vol, vp)
    transpose_planes(0, 3, 2 * ch)

    mine = pl.ds(pl.multiple_of(core * half, half), half)
    other = pl.ds(pl.multiple_of((1 - core) * half, half), half)

    def root(j):
        return (line - 1) // 2 + lax.rem(j, 2) * (line // 2 - (line - 1) // 2)

    def to_sibling(j):
        return remote(acc.at[:, j, other], r_sib.at[j], s_sib.at[j], r_sibs.at[j], sib)

    def line_up(j):
        return remote(acc.at[:, j, mine], r_lo.at[j], s_line.at[j], r_los.at[j], zhi)

    def line_down(j):
        return remote(acc.at[:, j, mine], r_hi.at[j], s_line.at[j], r_his.at[j], zlo)

    def across(j, k):
        return remote(acc.at[:, j, mine], r_y.at[k - 1, j], s_y.at[k - 1, j], r_ys.at[k - 1, j], peer(k))

    def final_up(j):
        return remote(fin.at[:, j, mine], fin.at[:, j, mine], s_up.at[j], r_fin.at[j], zhi)

    def final_down(j):
        return remote(fin.at[:, j, mine], fin.at[:, j, mine], s_dn.at[j], r_fin.at[j], zlo)

    def final_sibling(j):
        return remote(fin.at[:, j, mine], fin.at[:, j, mine], s_fs.at[j], r_fsib.at[j], sib)

    def stage_send(j):
        full = products(j, 2 * ch)
        acc[0, j] = acc[0, j] + full[:ch, :ch]
        acc[2, j] = acc[2, j] + full[ch:, ch:]
        to_sibling(j).start()

    def stage_sibling(j):
        to_sibling(j).wait_recv()
        acc[:, j, mine, :] = acc[:, j, mine, :] + r_sib[j]

        @pl.when(jnp.logical_and(z == 0, root(j) != 0))
        def _():
            line_up(j).start()

        @pl.when(jnp.logical_and(z == line - 1, root(j) != line - 1))
        def _():
            line_down(j).start()

    def stage_line(j):
        @pl.when(jnp.logical_and(z > 0, z < root(j)))
        def _():
            line_up(j).wait_recv()
            acc[:, j, mine, :] = acc[:, j, mine, :] + r_lo[j]
            line_up(j).start()

        @pl.when(jnp.logical_and(z < line - 1, z > root(j)))
        def _():
            line_down(j).wait_recv()
            acc[:, j, mine, :] = acc[:, j, mine, :] + r_hi[j]
            line_down(j).start()

    def stage_root(j):
        @pl.when(z == root(j))
        def _():
            @pl.when(has_lo)
            def _():
                line_up(j).wait_recv()
                acc[:, j, mine, :] = acc[:, j, mine, :] + r_lo[j]

            @pl.when(has_hi)
            def _():
                line_down(j).wait_recv()
                acc[:, j, mine, :] = acc[:, j, mine, :] + r_hi[j]

            for k in range(1, cols):
                across(j, k).start()

    def stage_across(j):
        @pl.when(z == root(j))
        def _():
            for k in range(1, cols):
                across(j, k).wait_recv()
            if cols <= 2:
                total = acc[:, j, mine, :]
                for k in range(1, cols):
                    total = total + r_y[k - 1, j]
            else:
                total = jnp.zeros((3, half, ch), F32)
                for i in range(cols):
                    term = acc[:, j, mine, :]
                    for k in range(1, cols):
                        term = jnp.where(lax.rem(y + cols - k, cols) == i, r_y[k - 1, j], term)
                    total = total + term
            fin[:, j, mine, :] = total * factor

            @pl.when(has_lo)
            def _():
                final_down(j).start()

            @pl.when(has_hi)
            def _():
                final_up(j).start()

            final_sibling(j).start()

    def stage_spread(j):
        @pl.when(z < root(j))
        def _():
            final_down(j).wait_recv()

            @pl.when(has_lo)
            def _():
                final_down(j).start()

            final_sibling(j).start()

        @pl.when(z > root(j))
        def _():
            final_up(j).wait_recv()

            @pl.when(has_hi)
            def _():
                final_up(j).start()

            final_sibling(j).start()

    def conv_tile(planes, weights, out, k, backward):
        start = k * rows
        bands = []
        for b in range(3):
            at = pl.ds(pl.multiple_of(start + b * breadth, 16), rows)
            for p in range(4):
                bands.append(planes[p, at, :])
        lhs = jnp.concatenate(bands, axis=1)
        sums = []
        for c in range(3):
            if backward:
                rhs = jnp.concatenate([weights[2 - b, 2 - c] for b in range(3)], axis=1)
                sums.append(lax.dot_general(
                    lhs, rhs, (((1,), (1,)), ((), ())), preferred_element_type=F32))
            else:
                rhs = jnp.concatenate([weights[b, c] for b in range(3)], axis=0)
                sums.append(jnp.dot(lhs, rhs, preferred_element_type=F32))
        total = (sums[1] + before_of(sums[0]) + after_of(sums[2])).astype(BF16)
        at = pl.ds(pl.multiple_of(start, 16), rows)
        out[0, at, :] = total[:, :ch]
        out[1, at, :] = total[:, ch:]

    for copy in wloads:
        copy.wait()

    def during(j, stage):
        @pl.when(jnp.logical_and(j >= 0, j < taps))
        def _():
            stage(j)

    lags = (
        (6, stage_spread), (4, stage_across), (3, stage_root),
        (2, stage_line), (1, stage_sibling), (0, stage_send),
    )
    steps = max(taps + 6, 2 * tiles)

    def step(s, carry):
        for lag, stage in lags:
            during(s - lag, stage)

        @pl.when(s < tiles)
        def _():
            conv_tile(vp, wf, act, s, False)

        @pl.when(s == tiles)
        def _():
            halo_wait(1, grd, gp)

        @pl.when(jnp.logical_and(s >= tiles, s < 2 * tiles))
        def _():
            conv_tile(gp, wb, ing, s - tiles, True)
        return carry

    lax.fori_loop(0, steps, step, 0)

    act_copy = pltpu.make_async_copy(act, act_out, s_out.at[0])
    ing_copy = pltpu.make_async_copy(ing, ing_out, s_out.at[1])
    dw_copy = pltpu.make_async_copy(fin, dw_out, s_out.at[2])
    act_copy.start()
    ing_copy.start()

    def finish(j, carry):
        to_sibling(j).wait_send()
        final_sibling(j).wait_send()

        @pl.when(z != root(j))
        def _():
            line_up(j).wait_send()

        @pl.when(z == root(j))
        def _():
            for k in range(1, cols):
                across(j, k).wait_send()

        @pl.when(jnp.logical_and(has_lo, z <= root(j)))
        def _():
            final_down(j).wait_send()

        @pl.when(jnp.logical_and(has_hi, z >= root(j)))
        def _():
            final_up(j).wait_send()

        final_sibling(j).wait_recv()
        return carry

    lax.fori_loop(0, taps, finish, 0)
    dw_copy.start()

    for which, src, dst in ((0, vol, vp), (1, grd, gp)):
        @pl.when(has_after)
        def _(which=which, src=src, dst=dst):
            halo(which, src, dst, True).wait_send()

        @pl.when(has_before)
        def _(which=which, src=src, dst=dst):
            halo(which, src, dst, False).wait_send()

    act_copy.wait()
    ing_copy.wait()
    dw_copy.wait()


def body(n, line, cols, volume, kernel, grad_out):
    planes, height, breadth, ch = volume.shape
    cells = height * breadth
    half = ch // 2
    taps = 9
    tile = 8
    factor = float(np.float32(1.0) / np.sqrt(np.float32(n * planes * cells)))
    dma = pltpu.SemaphoreType.DMA
    peers = max(cols - 1, 1)
    flops = 3 * 2 * 27 * planes * cells * ch * ch
    outs = pl.pallas_call(
        functools.partial(layer_kernel, n, line, cols, height, breadth, ch, tile, factor),
        out_shape=(
            jax.ShapeDtypeStruct((planes, cells, ch), BF16),
            jax.ShapeDtypeStruct((planes, cells, ch), BF16),
            jax.ShapeDtypeStruct((3, taps, ch, ch), F32),
        ),
        in_specs=[pl.BlockSpec(memory_space=pl.ANY)] * 3,
        out_specs=[pl.BlockSpec(memory_space=pl.ANY)] * 3,
        scratch_shapes=[
            pltpu.VMEM((4, cells + 2 * breadth, ch), BF16),
            pltpu.VMEM((4, cells + 2 * breadth, ch), BF16),
            pltpu.VMEM((3, 3, 4 * ch, 2 * ch), BF16),
            pltpu.VMEM((3, 3, 2 * ch, 4 * ch), BF16),
            pltpu.VMEM((4 * ch, cells), BF16),
            pltpu.VMEM((3, cells + 2 * breadth, 2 * ch), BF16),
            pltpu.VMEM((3, taps, ch, ch), F32),
            pltpu.VMEM((3, taps, ch, ch), F32),
            pltpu.VMEM((taps, 3, half, ch), F32),
            pltpu.VMEM((taps, 3, half, ch), F32),
            pltpu.VMEM((taps, 3, half, ch), F32),
            pltpu.VMEM((peers, taps, 3, half, ch), F32),
            pltpu.VMEM((planes, cells, ch), BF16),
            pltpu.VMEM((planes, cells, ch), BF16),
            dma((4,)), dma((2, 3, 2)), dma((2, 2)), dma((2, 2)),
            dma((taps,)), dma((taps,)), dma((taps,)), dma((taps,)), dma((taps,)),
            dma((peers, taps)), dma((peers, taps)),
            dma((taps,)), dma((taps,)), dma((taps,)), dma((taps,)), dma((taps,)),
            dma((3,)),
        ],
        compiler_params=pltpu.CompilerParams(
            collective_id=0, has_side_effects=True, vmem_limit_bytes=56 * 1024 * 1024),
        cost_estimate=pl.CostEstimate(flops=flops, bytes_accessed=10_000_000, transcendentals=0),
    )(
        volume.reshape(planes, cells, ch),
        kernel,
        grad_out.reshape(planes, cells, ch),
    )
    activation = outs[0].reshape(volume.shape)
    input_grad = outs[1].reshape(volume.shape)
    return activation, input_grad, outs[2].reshape(3, 3, 3, ch, ch)


def solution(mesh):
    n = mesh.shape["slab"]
    chips = n // 2
    cols = 1
    while cols * cols * 4 <= chips:
        cols *= 2
    line = chips // cols
    return jax.shard_map(
        functools.partial(body, n, line, cols),
        mesh=mesh,
        in_specs=(
            P(("groups", "slab"), None, None, None),
            P(),
            P(("groups", "slab"), None, None, None),
        ),
        out_specs=(
            P(("groups", "slab"), None, None, None),
            P(("groups", "slab"), None, None, None),
            P("groups", None, None, None, None),
        ),
        check_vma=False,
    )
```

```python
import functools

import jax
import jax.numpy as jnp
import numpy as np
from jax import lax
from jax.experimental import pallas as pl
from jax.experimental.pallas import tpu as pltpu
from jax.sharding import PartitionSpec as P

MESH = pl.DeviceIdType.MESH
F32 = jnp.float32
BF16 = jnp.bfloat16


def layer_kernel(
    n, line, cols, height, breadth, ch, tile, factor,
    vol, ker, grd,
    act_out, ing_out, dw_out,
    vp, gp, wf, wb, xt, gs, acc, fin, r_sib, r_lo, r_hi, r_y, act, ing,
    s_in, s_w, s_hs, s_hr, s_sib, r_sibs, s_line, r_los, r_his, s_y, r_ys,
    s_up, s_dn, s_fs, r_fin, r_fsib, s_out,
):
    cells = height * breadth
    half = ch // 2
    taps = 9
    me = lax.axis_index("slab")
    core = lax.rem(me, 2)
    chip = me // 2
    z = chip // cols
    y = lax.rem(chip, cols)
    sib = me + 1 - 2 * core
    zlo = me - 2 * cols
    zhi = me + 2 * cols
    has_lo, has_hi = z > 0, z < line - 1
    has_before, has_after = me > 0, me < n - 1

    def peer(k):
        return (z * cols + lax.rem(y + k, cols)) * 2 + core

    inner = pl.ds(breadth, cells)
    loads = []
    for p in range(2):
        loads.append(pltpu.make_async_copy(vol.at[p], vp.at[p + 1, inner], s_in.at[p]))
    for p in range(2):
        loads.append(pltpu.make_async_copy(grd.at[p], gp.at[p + 1, inner], s_in.at[p + 2]))
    for copy in loads:
        copy.start()
    wloads = []
    for c in range(3):
        wloads.append(pltpu.make_async_copy(
            ker.at[:, :, c], wf.at[:, :, :, pl.ds(c * ch, ch)], s_w.at[0, c]))
    for a in range(3):
        for b in range(3):
            wloads.append(pltpu.make_async_copy(
                ker.at[a, b], wb.at[:, :, pl.ds((8 - 3 * a - b) * ch, ch)], s_w.at[1 + a, b]))
    for copy in wloads:
        copy.start()

    barrier = pltpu.get_barrier_semaphore()

    def greet(dev):
        pl.semaphore_signal(barrier, inc=1, device_id={"slab": dev}, device_id_type=MESH)

    for k in range(1, cols):
        greet(peer(k))
    for cond, dev in ((has_before, me - 1), (has_after, me + 1), (has_lo, zlo), (has_hi, zhi)):
        @pl.when(cond)
        def _(dev=dev):
            greet(dev)
    partners = cols - 1
    for cond in (has_before, has_after, has_lo, has_hi):
        partners = partners + cond.astype(jnp.int32)
    pl.semaphore_wait(barrier, partners)

    def remote(src, dst, ssem, rsem, dev):
        return pltpu.make_async_remote_copy(
            src_ref=src, dst_ref=dst, send_sem=ssem, recv_sem=rsem,
            device_id={"slab": dev}, device_id_type=MESH)

    off_chip = jnp.where(core == 0, has_before, has_after)
    off_dev = me - 1 + 2 * core
    inside = 1 - core
    slot_sib, slot_off = 3 * inside, 3 * core

    def halo_sibling(which, src, dst):
        return remote(src.at[inside], dst.at[3 * core, inner], s_hs.at[which, 0], s_hr.at[which, 0], sib)

    def halo_off(which, src, dst):
        return remote(src.at[core], dst.at[3 * inside, inner], s_hs.at[which, 1], s_hr.at[which, 1], off_dev)

    def await_sibling(which, src, dst):
        remote(src.at[inside], dst.at[slot_sib, inner], s_hs.at[which, 0], s_hr.at[which, 0], sib).wait_recv()

    def await_off(which, src, dst):
        @pl.when(off_chip)
        def _():
            remote(src.at[core], dst.at[slot_off, inner], s_hs.at[which, 1], s_hr.at[which, 1], off_dev).wait_recv()

    @pl.when(off_chip)
    def _():
        halo_off(0, vol, vp).start()

    halo_sibling(0, vol, vp).start()
    halo_sibling(1, grd, gp).start()

    edge = jnp.zeros((breadth, ch), BF16)
    for ref in (vp, gp):
        for p in range(4):
            ref[p, pl.ds(0, breadth), :] = edge
            ref[p, pl.ds(breadth + cells, breadth), :] = edge
    for c in range(3):
        for d in range(2):
            gs[c, d, pl.ds(0, breadth), :] = edge
            gs[c, d, pl.ds(breadth + cells, breadth), :] = edge
    for cond, p in ((me == 0, 0), (me == n - 1, 3)):
        @pl.when(cond)
        def _(p=p):
            vp[p, inner, :] = jnp.zeros((cells, ch), BF16)
            gp[p, inner, :] = jnp.zeros((cells, ch), BF16)

    rows = tile * breadth
    tiles = height // tile
    column = lax.rem(lax.broadcasted_iota(jnp.int32, (rows, ch), 0), breadth)

    def before_of(v):
        return jnp.where(column == 0, 0.0, pltpu.roll(v, 1, 0))

    def after_of(v):
        return jnp.where(column == breadth - 1, 0.0, pltpu.roll(v, rows - 1, 0))

    for copy in loads:
        copy.wait()

    def shift_tile(k, carry):
        at = pl.ds(pl.multiple_of(breadth + k * rows, 16), rows)
        for d in range(2):
            plane = gp[d + 1, at, :]
            wide = plane.astype(F32)
            gs[0, d, at, :] = after_of(wide).astype(BF16)
            gs[1, d, at, :] = plane
            gs[2, d, at, :] = before_of(wide).astype(BF16)
        return carry

    lax.fori_loop(0, tiles, shift_tile, 0)

    def transpose_planes(pairs):
        def one(j, carry):
            at = pl.ds(pl.multiple_of(breadth + j * ch, 16), ch)
            to = pl.ds(pl.multiple_of(j * ch, ch), ch)
            for p, row in pairs:
                xt[pl.ds(row * ch, ch), to] = vp[p, at, :].T
            return carry
        lax.fori_loop(0, cells // ch, one, 0)

    def grads(t, d):
        b, c = t // 3, lax.rem(t, 3)
        return gs[c, d, pl.ds(pl.multiple_of((2 - b) * breadth, 16), cells), :]

    await_sibling(0, vol, vp)
    transpose_planes(((1, 0), (2, 1), (slot_sib, 2)))

    def own_part(t, carry):
        rhs = jnp.concatenate([grads(t, 0), grads(t, 1)], axis=1)
        full = jnp.dot(xt[pl.ds(0, 3 * ch), :], rhs, preferred_element_type=F32)
        beside = full[2 * ch:]
        acc[0, t] = full[:ch, ch:] + jnp.where(core == 1, beside[:, :ch], 0.0)
        acc[1, t] = full[:ch, :ch] + full[ch:2 * ch, ch:]
        acc[2, t] = full[ch:2 * ch, :ch] + jnp.where(core == 0, beside[:, ch:], 0.0)
        return carry

    lax.fori_loop(0, taps, own_part, 0)

    def conv_tile(planes, weights, out, d, k, backward):
        start = k * rows
        bands = []
        for a in range(3):
            for b in range(3):
                at = pl.ds(pl.multiple_of(start + b * breadth, 16), rows)
                bands.append(planes[d + a, at, :])
        lhs = jnp.concatenate(bands, axis=1)
        if backward:
            rhs = jnp.concatenate([weights[c] for c in range(3)], axis=0)
            sums = lax.dot_general(lhs, rhs, (((1,), (1,)), ((), ())), preferred_element_type=F32)
            first, last = sums[:, 2 * ch:], sums[:, :ch]
        else:
            rhs = jnp.concatenate([weights[a, b] for a in range(3) for b in range(3)], axis=0)
            sums = jnp.dot(lhs, rhs, preferred_element_type=F32)
            first, last = sums[:, :ch], sums[:, 2 * ch:]
        total = sums[:, ch:2 * ch] + before_of(first) + after_of(last)
        out[d, pl.ds(pl.multiple_of(start, 16), rows), :] = total.astype(BF16)

    for copy in wloads:
        copy.wait()

    def inside_act(k, carry):
        conv_tile(vp, wf, act, inside, k, False)
        return carry

    def inside_ing(k, carry):
        conv_tile(gp, wb, ing, inside, k, True)
        return carry

    lax.fori_loop(0, tiles, inside_act, 0)
    await_sibling(1, grd, gp)
    lax.fori_loop(0, tiles, inside_ing, 0)

    await_off(0, vol, vp)

    @pl.when(off_chip)
    def _():
        halo_off(1, grd, gp).start()

    transpose_planes(((slot_off, 3),))

    mine = pl.ds(pl.multiple_of(core * half, half), half)
    other = pl.ds(pl.multiple_of((1 - core) * half, half), half)

    def root(j):
        return (line - 1) // 2 + lax.rem(j, 2) * (line // 2 - (line - 1) // 2)

    def to_sibling(j):
        return remote(acc.at[:, j, other], r_sib.at[j], s_sib.at[j], r_sibs.at[j], sib)

    def line_up(j):
        return remote(acc.at[:, j, mine], r_lo.at[j], s_line.at[j], r_los.at[j], zhi)

    def line_down(j):
        return remote(acc.at[:, j, mine], r_hi.at[j], s_line.at[j], r_his.at[j], zlo)

    def across(j, k):
        return remote(acc.at[:, j, mine], r_y.at[k - 1, j], s_y.at[k - 1, j], r_ys.at[k - 1, j], peer(k))

    def final_up(j):
        return remote(fin.at[:, j, mine], fin.at[:, j, mine], s_up.at[j], r_fin.at[j], zhi)

    def final_down(j):
        return remote(fin.at[:, j, mine], fin.at[:, j, mine], s_dn.at[j], r_fin.at[j], zlo)

    def final_sibling(j):
        return remote(fin.at[:, j, mine], fin.at[:, j, mine], s_fs.at[j], r_fsib.at[j], sib)

    def stage_send(j):
        part = jnp.dot(xt[pl.ds(3 * ch, ch), :], grads(j, core), preferred_element_type=F32)
        acc[2 * core, j] = acc[2 * core, j] + part
        to_sibling(j).start()

    def stage_sibling(j):
        to_sibling(j).wait_recv()
        acc[:, j, mine, :] = acc[:, j, mine, :] + r_sib[j]

        @pl.when(jnp.logical_and(z == 0, root(j) != 0))
        def _():
            line_up(j).start()

        @pl.when(jnp.logical_and(z == line - 1, root(j) != line - 1))
        def _():
            line_down(j).start()

    def stage_line(j):
        @pl.when(jnp.logical_and(z > 0, z < root(j)))
        def _():
            line_up(j).wait_recv()
            acc[:, j, mine, :] = acc[:, j, mine, :] + r_lo[j]
            line_up(j).start()

        @pl.when(jnp.logical_and(z < line - 1, z > root(j)))
        def _():
            line_down(j).wait_recv()
            acc[:, j, mine, :] = acc[:, j, mine, :] + r_hi[j]
            line_down(j).start()

    def stage_root(j):
        @pl.when(z == root(j))
        def _():
            @pl.when(has_lo)
            def _():
                line_up(j).wait_recv()
                acc[:, j, mine, :] = acc[:, j, mine, :] + r_lo[j]

            @pl.when(has_hi)
            def _():
                line_down(j).wait_recv()
                acc[:, j, mine, :] = acc[:, j, mine, :] + r_hi[j]

            for k in range(1, cols):
                across(j, k).start()

    def stage_across(j):
        @pl.when(z == root(j))
        def _():
            for k in range(1, cols):
                across(j, k).wait_recv()
            if cols <= 2:
                total = acc[:, j, mine, :]
                for k in range(1, cols):
                    total = total + r_y[k - 1, j]
            else:
                total = jnp.zeros((3, half, ch), F32)
                for i in range(cols):
                    term = acc[:, j, mine, :]
                    for k in range(1, cols):
                        term = jnp.where(lax.rem(y + cols - k, cols) == i, r_y[k - 1, j], term)
                    total = total + term
            fin[:, j, mine, :] = total * factor

            @pl.when(has_lo)
            def _():
                final_down(j).start()

            @pl.when(has_hi)
            def _():
                final_up(j).start()

            final_sibling(j).start()

    def stage_spread(j):
        @pl.when(z < root(j))
        def _():
            final_down(j).wait_recv()

            @pl.when(has_lo)
            def _():
                final_down(j).start()

            final_sibling(j).start()

        @pl.when(z > root(j))
        def _():
            final_up(j).wait_recv()

            @pl.when(has_hi)
            def _():
                final_up(j).start()

            final_sibling(j).start()

    def during(j, stage):
        @pl.when(jnp.logical_and(j >= 0, j < taps))
        def _():
            stage(j)

    lags = (
        (6, stage_spread), (4, stage_across), (3, stage_root),
        (2, stage_line), (1, stage_sibling), (0, stage_send),
    )
    steps = max(taps + 6, 2 * tiles)

    def step(s, carry):
        for lag, stage in lags:
            during(s - lag, stage)

        @pl.when(s < tiles)
        def _():
            conv_tile(vp, wf, act, core, s, False)

        @pl.when(s == tiles)
        def _():
            await_off(1, grd, gp)

        @pl.when(jnp.logical_and(s >= tiles, s < 2 * tiles))
        def _():
            conv_tile(gp, wb, ing, core, s - tiles, True)
        return carry

    lax.fori_loop(0, steps, step, 0)

    act_copy = pltpu.make_async_copy(act, act_out, s_out.at[0])
    ing_copy = pltpu.make_async_copy(ing, ing_out, s_out.at[1])
    dw_copy = pltpu.make_async_copy(fin, dw_out, s_out.at[2])
    act_copy.start()
    ing_copy.start()

    def finish(j, carry):
        to_sibling(j).wait_send()
        final_sibling(j).wait_send()

        @pl.when(z != root(j))
        def _():
            line_up(j).wait_send()

        @pl.when(z == root(j))
        def _():
            for k in range(1, cols):
                across(j, k).wait_send()

        @pl.when(jnp.logical_and(has_lo, z <= root(j)))
        def _():
            final_down(j).wait_send()

        @pl.when(jnp.logical_and(has_hi, z >= root(j)))
        def _():
            final_up(j).wait_send()

        final_sibling(j).wait_recv()
        return carry

    lax.fori_loop(0, taps, finish, 0)
    dw_copy.start()

    for which, src, dst in ((0, vol, vp), (1, grd, gp)):
        halo_sibling(which, src, dst).wait_send()

        @pl.when(off_chip)
        def _(which=which, src=src, dst=dst):
            halo_off(which, src, dst).wait_send()

    act_copy.wait()
    ing_copy.wait()
    dw_copy.wait()


def body(n, line, cols, volume, kernel, grad_out):
    planes, height, breadth, ch = volume.shape
    cells = height * breadth
    half = ch // 2
    taps = 9
    tile = 8
    factor = float(np.float32(1.0) / np.sqrt(np.float32(n * planes * cells)))
    dma = pltpu.SemaphoreType.DMA
    peers = max(cols - 1, 1)
    flops = 3 * 2 * 27 * planes * cells * ch * ch
    outs = pl.pallas_call(
        functools.partial(layer_kernel, n, line, cols, height, breadth, ch, tile, factor),
        out_shape=(
            jax.ShapeDtypeStruct((planes, cells, ch), BF16),
            jax.ShapeDtypeStruct((planes, cells, ch), BF16),
            jax.ShapeDtypeStruct((3, taps, ch, ch), F32),
        ),
        in_specs=[pl.BlockSpec(memory_space=pl.ANY)] * 3,
        out_specs=[pl.BlockSpec(memory_space=pl.ANY)] * 3,
        scratch_shapes=[
            pltpu.VMEM((4, cells + 2 * breadth, ch), BF16),
            pltpu.VMEM((4, cells + 2 * breadth, ch), BF16),
            pltpu.VMEM((3, 3, ch, 3 * ch), BF16),
            pltpu.VMEM((3, ch, 9 * ch), BF16),
            pltpu.VMEM((4 * ch, cells), BF16),
            pltpu.VMEM((3, 2, cells + 2 * breadth, ch), BF16),
            pltpu.VMEM((3, taps, ch, ch), F32),
            pltpu.VMEM((3, taps, ch, ch), F32),
            pltpu.VMEM((taps, 3, half, ch), F32),
            pltpu.VMEM((taps, 3, half, ch), F32),
            pltpu.VMEM((taps, 3, half, ch), F32),
            pltpu.VMEM((peers, taps, 3, half, ch), F32),
            pltpu.VMEM((planes, cells, ch), BF16),
            pltpu.VMEM((planes, cells, ch), BF16),
            dma((4,)), dma((4, 3)), dma((2, 2)), dma((2, 2)),
            dma((taps,)), dma((taps,)), dma((taps,)), dma((taps,)), dma((taps,)),
            dma((peers, taps)), dma((peers, taps)),
            dma((taps,)), dma((taps,)), dma((taps,)), dma((taps,)), dma((taps,)),
            dma((3,)),
        ],
        compiler_params=pltpu.CompilerParams(
            collective_id=0, has_side_effects=True, vmem_limit_bytes=56 * 1024 * 1024),
        cost_estimate=pl.CostEstimate(flops=flops, bytes_accessed=10_000_000, transcendentals=0),
    )(
        volume.reshape(planes, cells, ch),
        kernel,
        grad_out.reshape(planes, cells, ch),
    )
    activation = outs[0].reshape(volume.shape)
    input_grad = outs[1].reshape(volume.shape)
    return activation, input_grad, outs[2].reshape(3, 3, 3, ch, ch)


def solution(mesh):
    n = mesh.shape["slab"]
    chips = n // 2
    cols = 1
    while cols * cols * 4 <= chips:
        cols *= 2
    line = chips // cols
    return jax.shard_map(
        functools.partial(body, n, line, cols),
        mesh=mesh,
        in_specs=(
            P(("groups", "slab"), None, None, None),
            P(),
            P(("groups", "slab"), None, None, None),
        ),
        out_specs=(
            P(("groups", "slab"), None, None, None),
            P(("groups", "slab"), None, None, None),
            P("groups", None, None, None, None),
        ),
        check_vma=False,
    )
```

```python
import functools

import jax
import jax.numpy as jnp
import numpy as np
from jax import lax
from jax.experimental import pallas as pl
from jax.experimental.pallas import tpu as pltpu
from jax.sharding import PartitionSpec as P

MESH = pl.DeviceIdType.MESH
F32 = jnp.float32
BF16 = jnp.bfloat16


def layer_kernel(
    n, line, cols, height, breadth, ch, tile, factor,
    vol, grd,
    vh_out, gh_out, dw_out,
    vp, gp, xt, gs, acc, fin, r_sib, r_lo, r_hi, r_y,
    s_in, s_hs, s_hr, s_sib, r_sibs, s_line, r_los, r_his, s_y, r_ys,
    s_up, s_dn, s_fs, r_fin, r_fsib, s_out,
):
    cells = height * breadth
    half = ch // 2
    taps = 9
    me = lax.axis_index("slab")
    core = lax.rem(me, 2)
    chip = me // 2
    z = chip // cols
    y = lax.rem(chip, cols)
    sib = me + 1 - 2 * core
    zlo = me - 2 * cols
    zhi = me + 2 * cols
    has_lo, has_hi = z > 0, z < line - 1
    has_before, has_after = me > 0, me < n - 1

    def peer(k):
        return (z * cols + lax.rem(y + k, cols)) * 2 + core

    inner = pl.ds(breadth, cells)
    loads = []
    for p in range(2):
        loads.append(pltpu.make_async_copy(vol.at[p], vp.at[p + 1, inner], s_in.at[p]))
    for p in range(2):
        loads.append(pltpu.make_async_copy(grd.at[p], gp.at[p + 1, inner], s_in.at[p + 2]))
    for copy in loads:
        copy.start()
    barrier = pltpu.get_barrier_semaphore()

    def greet(dev):
        pl.semaphore_signal(barrier, inc=1, device_id={"slab": dev}, device_id_type=MESH)

    for k in range(1, cols):
        greet(peer(k))
    for cond, dev in ((has_before, me - 1), (has_after, me + 1), (has_lo, zlo), (has_hi, zhi)):
        @pl.when(cond)
        def _(dev=dev):
            greet(dev)
    partners = cols - 1
    for cond in (has_before, has_after, has_lo, has_hi):
        partners = partners + cond.astype(jnp.int32)
    pl.semaphore_wait(barrier, partners)

    def remote(src, dst, ssem, rsem, dev):
        return pltpu.make_async_remote_copy(
            src_ref=src, dst_ref=dst, send_sem=ssem, recv_sem=rsem,
            device_id={"slab": dev}, device_id_type=MESH)

    off_chip = jnp.where(core == 0, has_before, has_after)
    off_dev = me - 1 + 2 * core
    inside = 1 - core
    slot_sib, slot_off = 3 * inside, 3 * core

    def halo_sibling(which, src, dst):
        return remote(src.at[inside], dst.at[3 * core, inner], s_hs.at[which, 0], s_hr.at[which, 0], sib)

    def halo_off(which, src, dst):
        return remote(src.at[core], dst.at[3 * inside, inner], s_hs.at[which, 1], s_hr.at[which, 1], off_dev)

    def await_sibling(which, src, dst):
        remote(src.at[inside], dst.at[slot_sib, inner], s_hs.at[which, 0], s_hr.at[which, 0], sib).wait_recv()

    def await_off(which, src, dst):
        @pl.when(off_chip)
        def _():
            remote(src.at[core], dst.at[slot_off, inner], s_hs.at[which, 1], s_hr.at[which, 1], off_dev).wait_recv()

    @pl.when(off_chip)
    def _():
        halo_off(0, vol, vp).start()

    halo_sibling(0, vol, vp).start()
    halo_sibling(1, grd, gp).start()

    edge = jnp.zeros((breadth, ch), BF16)
    for ref in (vp, gp):
        for p in range(4):
            ref[p, pl.ds(0, breadth), :] = edge
            ref[p, pl.ds(breadth + cells, breadth), :] = edge
    for c in range(3):
        for d in range(2):
            gs[c, d, pl.ds(0, breadth), :] = edge
            gs[c, d, pl.ds(breadth + cells, breadth), :] = edge
    for cond, p in ((me == 0, 0), (me == n - 1, 3)):
        @pl.when(cond)
        def _(p=p):
            vp[p, inner, :] = jnp.zeros((cells, ch), BF16)
            gp[p, inner, :] = jnp.zeros((cells, ch), BF16)

    rows = tile * breadth
    tiles = height // tile
    column = lax.rem(lax.broadcasted_iota(jnp.int32, (rows, ch), 0), breadth)

    def before_of(v):
        return jnp.where(column == 0, 0.0, pltpu.roll(v, 1, 0))

    def after_of(v):
        return jnp.where(column == breadth - 1, 0.0, pltpu.roll(v, rows - 1, 0))

    for copy in loads:
        copy.wait()

    def shift_tile(k, carry):
        at = pl.ds(pl.multiple_of(breadth + k * rows, 16), rows)
        for d in range(2):
            plane = gp[d + 1, at, :]
            wide = plane.astype(F32)
            gs[0, d, at, :] = after_of(wide).astype(BF16)
            gs[1, d, at, :] = plane
            gs[2, d, at, :] = before_of(wide).astype(BF16)
        return carry

    lax.fori_loop(0, tiles, shift_tile, 0)

    def transpose_planes(pairs):
        def one(j, carry):
            at = pl.ds(pl.multiple_of(breadth + j * ch, 16), ch)
            to = pl.ds(pl.multiple_of(j * ch, ch), ch)
            for p, row in pairs:
                xt[pl.ds(row * ch, ch), to] = vp[p, at, :].T
            return carry
        lax.fori_loop(0, cells // ch, one, 0)

    def grads(t, d):
        b, c = t // 3, lax.rem(t, 3)
        return gs[c, d, pl.ds(pl.multiple_of((2 - b) * breadth, 16), cells), :]

    await_sibling(0, vol, vp)
    transpose_planes(((1, 0), (2, 1), (slot_sib, 2)))

    def own_part(t, carry):
        rhs = jnp.concatenate([grads(t, 0), grads(t, 1)], axis=1)
        full = jnp.dot(xt[pl.ds(0, 3 * ch), :], rhs, preferred_element_type=F32)
        beside = full[2 * ch:]
        acc[0, t] = full[:ch, ch:] + jnp.where(core == 1, beside[:, :ch], 0.0)
        acc[1, t] = full[:ch, :ch] + full[ch:2 * ch, ch:]
        acc[2, t] = full[ch:2 * ch, :ch] + jnp.where(core == 0, beside[:, ch:], 0.0)
        return carry

    lax.fori_loop(0, taps, own_part, 0)

    await_sibling(1, grd, gp)
    await_off(0, vol, vp)

    @pl.when(off_chip)
    def _():
        halo_off(1, grd, gp).start()

    transpose_planes(((slot_off, 3),))

    mine = pl.ds(pl.multiple_of(core * half, half), half)
    other = pl.ds(pl.multiple_of((1 - core) * half, half), half)

    def root(j):
        return (line - 1) // 2 + lax.rem(j, 2) * (line // 2 - (line - 1) // 2)

    def to_sibling(j):
        return remote(acc.at[:, j, other], r_sib.at[j], s_sib.at[j], r_sibs.at[j], sib)

    def line_up(j):
        return remote(acc.at[:, j, mine], r_lo.at[j], s_line.at[j], r_los.at[j], zhi)

    def line_down(j):
        return remote(acc.at[:, j, mine], r_hi.at[j], s_line.at[j], r_his.at[j], zlo)

    def across(j, k):
        return remote(acc.at[:, j, mine], r_y.at[k - 1, j], s_y.at[k - 1, j], r_ys.at[k - 1, j], peer(k))

    def final_up(j):
        return remote(fin.at[:, j, mine], fin.at[:, j, mine], s_up.at[j], r_fin.at[j], zhi)

    def final_down(j):
        return remote(fin.at[:, j, mine], fin.at[:, j, mine], s_dn.at[j], r_fin.at[j], zlo)

    def final_sibling(j):
        return remote(fin.at[:, j, mine], fin.at[:, j, mine], s_fs.at[j], r_fsib.at[j], sib)

    def stage_send(j):
        part = jnp.dot(xt[pl.ds(3 * ch, ch), :], grads(j, core), preferred_element_type=F32)
        acc[2 * core, j] = acc[2 * core, j] + part
        to_sibling(j).start()

    def stage_sibling(j):
        to_sibling(j).wait_recv()
        acc[:, j, mine, :] = acc[:, j, mine, :] + r_sib[j]

        @pl.when(jnp.logical_and(z == 0, root(j) != 0))
        def _():
            line_up(j).start()

        @pl.when(jnp.logical_and(z == line - 1, root(j) != line - 1))
        def _():
            line_down(j).start()

    def stage_line(j):
        @pl.when(jnp.logical_and(z > 0, z < root(j)))
        def _():
            line_up(j).wait_recv()
            acc[:, j, mine, :] = acc[:, j, mine, :] + r_lo[j]
            line_up(j).start()

        @pl.when(jnp.logical_and(z < line - 1, z > root(j)))
        def _():
            line_down(j).wait_recv()
            acc[:, j, mine, :] = acc[:, j, mine, :] + r_hi[j]
            line_down(j).start()

    def stage_root(j):
        @pl.when(z == root(j))
        def _():
            @pl.when(has_lo)
            def _():
                line_up(j).wait_recv()
                acc[:, j, mine, :] = acc[:, j, mine, :] + r_lo[j]

            @pl.when(has_hi)
            def _():
                line_down(j).wait_recv()
                acc[:, j, mine, :] = acc[:, j, mine, :] + r_hi[j]

            for k in range(1, cols):
                across(j, k).start()

    def stage_across(j):
        @pl.when(z == root(j))
        def _():
            for k in range(1, cols):
                across(j, k).wait_recv()
            if cols <= 2:
                total = acc[:, j, mine, :]
                for k in range(1, cols):
                    total = total + r_y[k - 1, j]
            else:
                total = jnp.zeros((3, half, ch), F32)
                for i in range(cols):
                    term = acc[:, j, mine, :]
                    for k in range(1, cols):
                        term = jnp.where(lax.rem(y + cols - k, cols) == i, r_y[k - 1, j], term)
                    total = total + term
            fin[:, j, mine, :] = total * factor

            @pl.when(has_lo)
            def _():
                final_down(j).start()

            @pl.when(has_hi)
            def _():
                final_up(j).start()

            final_sibling(j).start()

    def stage_spread(j):
        @pl.when(z < root(j))
        def _():
            final_down(j).wait_recv()

            @pl.when(has_lo)
            def _():
                final_down(j).start()

            final_sibling(j).start()

        @pl.when(z > root(j))
        def _():
            final_up(j).wait_recv()

            @pl.when(has_hi)
            def _():
                final_up(j).start()

            final_sibling(j).start()

    def during(j, stage):
        @pl.when(jnp.logical_and(j >= 0, j < taps))
        def _():
            stage(j)

    lags = (
        (6, stage_spread), (4, stage_across), (3, stage_root),
        (2, stage_line), (1, stage_sibling), (0, stage_send),
    )
    steps = taps + 6

    def step(s, carry):
        for lag, stage in lags:
            during(s - lag, stage)

        return carry

    lax.fori_loop(0, steps, step, 0)
    await_off(1, grd, gp)

    sides = []
    for i, (planes, out) in enumerate(((vp, vh_out), (gp, gh_out))):
        for k in range(2):
            sides.append(pltpu.make_async_copy(planes.at[3 * k, inner], out.at[k], s_out.at[1 + 2 * i + k]))
    for copy in sides:
        copy.start()
    dw_copy = pltpu.make_async_copy(fin, dw_out, s_out.at[0])

    def finish(j, carry):
        to_sibling(j).wait_send()
        final_sibling(j).wait_send()

        @pl.when(z != root(j))
        def _():
            line_up(j).wait_send()

        @pl.when(z == root(j))
        def _():
            for k in range(1, cols):
                across(j, k).wait_send()

        @pl.when(jnp.logical_and(has_lo, z <= root(j)))
        def _():
            final_down(j).wait_send()

        @pl.when(jnp.logical_and(has_hi, z >= root(j)))
        def _():
            final_up(j).wait_send()

        final_sibling(j).wait_recv()
        return carry

    lax.fori_loop(0, taps, finish, 0)
    dw_copy.start()

    for which, src, dst in ((0, vol, vp), (1, grd, gp)):
        halo_sibling(which, src, dst).wait_send()

        @pl.when(off_chip)
        def _(which=which, src=src, dst=dst):
            halo_off(which, src, dst).wait_send()

    for copy in sides:
        copy.wait()
    dw_copy.wait()


def load_planes(breadth, cells, ch, src, sides, planes, sem):
    inner = pl.ds(breadth, cells)
    copies = [pltpu.make_async_copy(src.at[k], planes.at[k + 1, inner], sem.at[k]) for k in range(2)]
    copies += [pltpu.make_async_copy(sides.at[k], planes.at[3 * k, inner], sem.at[2 + k]) for k in range(2)]
    for copy in copies:
        copy.start()
    edge = jnp.zeros((breadth, ch), BF16)
    for p in range(4):
        planes[p, pl.ds(0, breadth), :] = edge
        planes[p, pl.ds(breadth + cells, breadth), :] = edge
    return copies


def shifted_sum(breadth, first, middle, last):
    rows = first.shape[0]
    column = lax.rem(lax.broadcasted_iota(jnp.int32, first.shape, 0), breadth)
    before = jnp.where(column == 0, 0.0, pltpu.roll(first, 1, 0))
    after = jnp.where(column == breadth - 1, 0.0, pltpu.roll(last, rows - 1, 0))
    return (middle + before + after).astype(BF16)


def conv_pair(height, breadth, ch, tile, src, sides, ker, out, planes, w, sem):
    rows, tiles = tile * breadth, height // tile
    copies = load_planes(breadth, height * breadth, ch, src, sides, planes, sem)
    blank = jnp.zeros((3, 3, ch, ch), BF16)
    for p in range(4):
        for d in range(2):
            value = ker[p - d] if 0 <= p - d <= 2 else blank
            w[:, :, pl.ds(p * ch, ch), pl.ds(d * ch, ch)] = value
    for copy in copies:
        copy.wait()

    def one(k, carry):
        bands = []
        for b in range(3):
            at = pl.ds(pl.multiple_of(k * rows + b * breadth, 16), rows)
            bands += [planes[p, at, :] for p in range(4)]
        lhs = jnp.concatenate(bands, axis=1)
        sums = [
            jnp.dot(lhs, jnp.concatenate([w[b, c] for b in range(3)], axis=0), preferred_element_type=F32)
            for c in range(3)
        ]
        total = shifted_sum(breadth, *sums)
        at = pl.ds(pl.multiple_of(k * rows, 16), rows)
        out[0, at, :] = total[:, :ch]
        out[1, at, :] = total[:, ch:]
        return carry

    lax.fori_loop(0, tiles, one, 0)


def conv_single(height, breadth, ch, tile, src, sides, ker, out, planes, w, sem):
    rows, tiles = tile * breadth, height // tile
    copies = load_planes(breadth, height * breadth, ch, src, sides, planes, sem)
    for a in range(3):
        for b in range(3):
            for c in range(3):
                w[pl.ds((3 * a + b) * ch, ch), pl.ds(c * ch, ch)] = ker[2 - a, 2 - b, 2 - c].T
    for copy in copies:
        copy.wait()

    def one(i, carry):
        d, k = i // tiles, lax.rem(i, tiles)
        bands = []
        for a in range(3):
            for b in range(3):
                at = pl.ds(pl.multiple_of(k * rows + b * breadth, 16), rows)
                bands.append(planes[d + a, at, :])
        lhs = jnp.concatenate(bands, axis=1)
        sums = jnp.dot(lhs, w[...], preferred_element_type=F32)
        total = shifted_sum(breadth, *(sums[:, c * ch:(c + 1) * ch] for c in range(3)))
        out[d, pl.ds(pl.multiple_of(k * rows, 16), rows), :] = total
        return carry

    lax.fori_loop(0, 2 * tiles, one, 0)


def body(n, line, cols, volume, kernel, grad_out):
    planes, height, breadth, ch = volume.shape
    cells = height * breadth
    half = ch // 2
    taps = 9
    tile = 8
    factor = float(np.float32(1.0) / np.sqrt(np.float32(n * planes * cells)))
    dma = pltpu.SemaphoreType.DMA
    peers = max(cols - 1, 1)
    flops = 3 * 2 * 27 * planes * cells * ch * ch
    vol = volume.reshape(planes, cells, ch)
    grd = grad_out.reshape(planes, cells, ch)
    outs = pl.pallas_call(
        functools.partial(layer_kernel, n, line, cols, height, breadth, ch, tile, factor),
        out_shape=(
            jax.ShapeDtypeStruct((2, cells, ch), BF16),
            jax.ShapeDtypeStruct((2, cells, ch), BF16),
            jax.ShapeDtypeStruct((3, taps, ch, ch), F32),
        ),
        in_specs=[pl.BlockSpec(memory_space=pl.ANY)] * 2,
        out_specs=[pl.BlockSpec(memory_space=pl.ANY)] * 3,
        scratch_shapes=[
            pltpu.VMEM((4, cells + 2 * breadth, ch), BF16),
            pltpu.VMEM((4, cells + 2 * breadth, ch), BF16),
            pltpu.VMEM((4 * ch, cells), BF16),
            pltpu.VMEM((3, 2, cells + 2 * breadth, ch), BF16),
            pltpu.VMEM((3, taps, ch, ch), F32),
            pltpu.VMEM((3, taps, ch, ch), F32),
            pltpu.VMEM((taps, 3, half, ch), F32),
            pltpu.VMEM((taps, 3, half, ch), F32),
            pltpu.VMEM((taps, 3, half, ch), F32),
            pltpu.VMEM((peers, taps, 3, half, ch), F32),
            dma((4,)), dma((2, 2)), dma((2, 2)),
            dma((taps,)), dma((taps,)), dma((taps,)), dma((taps,)), dma((taps,)),
            dma((peers, taps)), dma((peers, taps)),
            dma((taps,)), dma((taps,)), dma((taps,)), dma((taps,)), dma((taps,)),
            dma((5,)),
        ],
        compiler_params=pltpu.CompilerParams(
            collective_id=0, has_side_effects=True, vmem_limit_bytes=56 * 1024 * 1024),
        cost_estimate=pl.CostEstimate(flops=flops, bytes_accessed=10_000_000, transcendentals=0),
    )(vol, grd)
    vmem = pl.BlockSpec(memory_space=pltpu.VMEM)
    padded_rows = cells + 2 * breadth

    def conv(kern, wshape):
        return pl.pallas_call(
            functools.partial(kern, height, breadth, ch, tile),
            out_shape=jax.ShapeDtypeStruct((planes, cells, ch), BF16),
            in_specs=[pl.BlockSpec(memory_space=pl.ANY), pl.BlockSpec(memory_space=pl.ANY), vmem],
            out_specs=vmem,
            scratch_shapes=[
                pltpu.VMEM((4, padded_rows, ch), BF16),
                pltpu.VMEM(wshape, BF16),
                dma((4,)),
            ],
            compiler_params=pltpu.CompilerParams(vmem_limit_bytes=40 * 1024 * 1024),
            cost_estimate=pl.CostEstimate(flops=flops // 3, bytes_accessed=5_000_000, transcendentals=0),
        )

    activation = conv(conv_pair, (3, 3, 4 * ch, 2 * ch))(vol, outs[0], kernel)
    input_grad = conv(conv_single, (9 * ch, 3 * ch))(grd, outs[1], kernel)
    return (
        activation.reshape(volume.shape), input_grad.reshape(volume.shape),
        outs[2].reshape(3, 3, 3, ch, ch),
    )


def solution(mesh):
    n = mesh.shape["slab"]
    chips = n // 2
    cols = 1
    while cols * cols * 4 <= chips:
        cols *= 2
    line = chips // cols
    return jax.shard_map(
        functools.partial(body, n, line, cols),
        mesh=mesh,
        in_specs=(
            P(("groups", "slab"), None, None, None),
            P(),
            P(("groups", "slab"), None, None, None),
        ),
        out_specs=(
            P(("groups", "slab"), None, None, None),
            P(("groups", "slab"), None, None, None),
            P("groups", None, None, None, None),
        ),
        check_vma=False,
    )
```

```python
import functools

import jax
import jax.numpy as jnp
import numpy as np
from jax import lax
from jax.experimental import pallas as pl
from jax.experimental.pallas import tpu as pltpu
from jax.sharding import PartitionSpec as P

MESH = pl.DeviceIdType.MESH
F32 = jnp.float32
BF16 = jnp.bfloat16


def layer_kernel(
    n, line, cols, height, breadth, ch, tile, factor,
    vol, ker, grd,
    act_out, ing_out, dw_out,
    vp, gp, wf, wk, wb, xt, gs, acc, fin, r_sib, r_lo, r_hi, r_y, act, ing,
    s_in, s_w, s_hs, s_hr, s_sib, r_sibs, s_line, r_los, r_his, s_y, r_ys,
    s_up, s_dn, s_fs, r_fin, r_fsib, s_out,
):
    cells = height * breadth
    half = ch // 2
    taps = 9
    me = lax.axis_index("slab")
    core = lax.rem(me, 2)
    chip = me // 2
    z = chip // cols
    y = lax.rem(chip, cols)
    sib = me + 1 - 2 * core
    zlo = me - 2 * cols
    zhi = me + 2 * cols
    has_lo, has_hi = z > 0, z < line - 1
    has_before, has_after = me > 0, me < n - 1

    def peer(k):
        return (z * cols + lax.rem(y + k, cols)) * 2 + core

    inner = pl.ds(breadth, cells)
    loads = []
    for p in range(2):
        loads.append(pltpu.make_async_copy(vol.at[p], vp.at[p + 1, inner], s_in.at[p]))
    for p in range(2):
        loads.append(pltpu.make_async_copy(grd.at[p], gp.at[p + 1, inner], s_in.at[p + 2]))
    for copy in loads:
        copy.start()
    wloads = []
    for c in range(3):
        wloads.append(pltpu.make_async_copy(
            ker.at[:, :, c], wf.at[:, :, :, pl.ds(c * ch, ch)], s_w.at[c]))
    wloads.append(pltpu.make_async_copy(ker, wk, s_w.at[3]))
    for copy in wloads:
        copy.start()

    barrier = pltpu.get_barrier_semaphore()

    def greet(dev):
        pl.semaphore_signal(barrier, inc=1, device_id={"slab": dev}, device_id_type=MESH)

    for k in range(1, cols):
        greet(peer(k))
    for cond, dev in ((has_before, me - 1), (has_after, me + 1), (has_lo, zlo), (has_hi, zhi)):
        @pl.when(cond)
        def _(dev=dev):
            greet(dev)
    partners = cols - 1
    for cond in (has_before, has_after, has_lo, has_hi):
        partners = partners + cond.astype(jnp.int32)
    pl.semaphore_wait(barrier, partners)

    def remote(src, dst, ssem, rsem, dev):
        return pltpu.make_async_remote_copy(
            src_ref=src, dst_ref=dst, send_sem=ssem, recv_sem=rsem,
            device_id={"slab": dev}, device_id_type=MESH)

    off_chip = jnp.where(core == 0, has_before, has_after)
    off_dev = me - 1 + 2 * core
    inside = 1 - core
    slot_sib, slot_off = 3 * inside, 3 * core

    def halo_sibling(which, src, dst):
        return remote(src.at[inside], dst.at[3 * core, inner], s_hs.at[which, 0], s_hr.at[which, 0], sib)

    def halo_off(which, src, dst):
        return remote(src.at[core], dst.at[3 * inside, inner], s_hs.at[which, 1], s_hr.at[which, 1], off_dev)

    def await_sibling(which, src, dst):
        remote(src.at[inside], dst.at[slot_sib, inner], s_hs.at[which, 0], s_hr.at[which, 0], sib).wait_recv()

    def await_off(which, src, dst):
        @pl.when(off_chip)
        def _():
            remote(src.at[core], dst.at[slot_off, inner], s_hs.at[which, 1], s_hr.at[which, 1], off_dev).wait_recv()

    @pl.when(off_chip)
    def _():
        halo_off(0, vol, vp).start()

    halo_sibling(0, vol, vp).start()
    halo_sibling(1, grd, gp).start()

    edge = jnp.zeros((breadth, ch), BF16)
    for ref in (vp, gp):
        for p in range(4):
            ref[p, pl.ds(0, breadth), :] = edge
            ref[p, pl.ds(breadth + cells, breadth), :] = edge
    for c in range(3):
        for d in range(2):
            gs[c, d, pl.ds(0, breadth), :] = edge
            gs[c, d, pl.ds(breadth + cells, breadth), :] = edge
    for cond, p in ((me == 0, 0), (me == n - 1, 3)):
        @pl.when(cond)
        def _(p=p):
            vp[p, inner, :] = jnp.zeros((cells, ch), BF16)
            gp[p, inner, :] = jnp.zeros((cells, ch), BF16)

    rows = tile * breadth
    tiles = height // tile
    column = lax.rem(lax.broadcasted_iota(jnp.int32, (rows, ch), 0), breadth)

    def before_of(v):
        return jnp.where(column == 0, 0.0, pltpu.roll(v, 1, 0))

    def after_of(v):
        return jnp.where(column == breadth - 1, 0.0, pltpu.roll(v, rows - 1, 0))

    for copy in loads:
        copy.wait()

    def shift_tile(k, carry):
        at = pl.ds(pl.multiple_of(breadth + k * rows, 16), rows)
        for d in range(2):
            plane = gp[d + 1, at, :]
            wide = plane.astype(F32)
            gs[0, d, at, :] = after_of(wide).astype(BF16)
            gs[1, d, at, :] = plane
            gs[2, d, at, :] = before_of(wide).astype(BF16)
        return carry

    lax.fori_loop(0, tiles, shift_tile, 0)

    def transpose_planes(pairs):
        def one(j, carry):
            at = pl.ds(pl.multiple_of(breadth + j * ch, 16), ch)
            to = pl.ds(pl.multiple_of(j * ch, ch), ch)
            for p, row in pairs:
                xt[pl.ds(row * ch, ch), to] = vp[p, at, :].T
            return carry
        lax.fori_loop(0, cells // ch, one, 0)

    def grads(t, d):
        b, c = t // 3, lax.rem(t, 3)
        return gs[c, d, pl.ds(pl.multiple_of((2 - b) * breadth, 16), cells), :]

    await_sibling(0, vol, vp)
    transpose_planes(((1, 0), (2, 1), (slot_sib, 2)))

    def own_part(t, carry):
        rhs = jnp.concatenate([grads(t, 0), grads(t, 1)], axis=1)
        full = jnp.dot(xt[pl.ds(0, 3 * ch), :], rhs, preferred_element_type=F32)
        beside = full[2 * ch:]
        acc[0, t] = full[:ch, ch:] + jnp.where(core == 1, beside[:, :ch], 0.0)
        acc[1, t] = full[:ch, :ch] + full[ch:2 * ch, ch:]
        acc[2, t] = full[ch:2 * ch, :ch] + jnp.where(core == 0, beside[:, ch:], 0.0)
        return carry

    lax.fori_loop(0, taps, own_part, 0)

    def conv_tile(planes, weights, out, d, k, backward):
        start = k * rows
        bands = []
        for a in range(3):
            for b in range(3):
                at = pl.ds(pl.multiple_of(start + b * breadth, 16), rows)
                bands.append(planes[d + a, at, :])
        lhs = jnp.concatenate(bands, axis=1)
        if backward:
            rhs = weights[...]
        else:
            rhs = jnp.concatenate([weights[a, b] for a in range(3) for b in range(3)], axis=0)
        sums = jnp.dot(lhs, rhs, preferred_element_type=F32)
        first, last = sums[:, :ch], sums[:, 2 * ch:]
        total = sums[:, ch:2 * ch] + before_of(first) + after_of(last)
        out[d, pl.ds(pl.multiple_of(start, 16), rows), :] = total.astype(BF16)

    for copy in wloads:
        copy.wait()
    for a in range(3):
        for b in range(3):
            for c in range(3):
                wb[pl.ds((3 * a + b) * ch, ch), pl.ds(c * ch, ch)] = wk[2 - a, 2 - b, 2 - c].T

    def inside_act(k, carry):
        conv_tile(vp, wf, act, inside, k, False)
        return carry

    def inside_ing(k, carry):
        conv_tile(gp, wb, ing, inside, k, True)
        return carry

    lax.fori_loop(0, tiles, inside_act, 0)
    await_sibling(1, grd, gp)
    lax.fori_loop(0, tiles, inside_ing, 0)

    await_off(0, vol, vp)

    @pl.when(off_chip)
    def _():
        halo_off(1, grd, gp).start()

    transpose_planes(((slot_off, 3),))

    mine = pl.ds(pl.multiple_of(core * half, half), half)
    other = pl.ds(pl.multiple_of((1 - core) * half, half), half)

    def root(j):
        return (line - 1) // 2 + lax.rem(j, 2) * (line // 2 - (line - 1) // 2)

    def to_sibling(j):
        return remote(acc.at[:, j, other], r_sib.at[j], s_sib.at[j], r_sibs.at[j], sib)

    def line_up(j):
        return remote(acc.at[:, j, mine], r_lo.at[j], s_line.at[j], r_los.at[j], zhi)

    def line_down(j):
        return remote(acc.at[:, j, mine], r_hi.at[j], s_line.at[j], r_his.at[j], zlo)

    def across(j, k):
        return remote(acc.at[:, j, mine], r_y.at[k - 1, j], s_y.at[k - 1, j], r_ys.at[k - 1, j], peer(k))

    def final_up(j):
        return remote(fin.at[:, j, mine], fin.at[:, j, mine], s_up.at[j], r_fin.at[j], zhi)

    def final_down(j):
        return remote(fin.at[:, j, mine], fin.at[:, j, mine], s_dn.at[j], r_fin.at[j], zlo)

    def final_sibling(j):
        return remote(fin.at[:, j, mine], fin.at[:, j, mine], s_fs.at[j], r_fsib.at[j], sib)

    def stage_send(j):
        part = jnp.dot(xt[pl.ds(3 * ch, ch), :], grads(j, core), preferred_element_type=F32)
        acc[2 * core, j] = acc[2 * core, j] + part
        to_sibling(j).start()

    def stage_sibling(j):
        to_sibling(j).wait_recv()
        acc[:, j, mine, :] = acc[:, j, mine, :] + r_sib[j]

        @pl.when(jnp.logical_and(z == 0, root(j) != 0))
        def _():
            line_up(j).start()

        @pl.when(jnp.logical_and(z == line - 1, root(j) != line - 1))
        def _():
            line_down(j).start()

    def stage_line(j):
        @pl.when(jnp.logical_and(z > 0, z < root(j)))
        def _():
            line_up(j).wait_recv()
            acc[:, j, mine, :] = acc[:, j, mine, :] + r_lo[j]
            line_up(j).start()

        @pl.when(jnp.logical_and(z < line - 1, z > root(j)))
        def _():
            line_down(j).wait_recv()
            acc[:, j, mine, :] = acc[:, j, mine, :] + r_hi[j]
            line_down(j).start()

    def stage_root(j):
        @pl.when(z == root(j))
        def _():
            @pl.when(has_lo)
            def _():
                line_up(j).wait_recv()
                acc[:, j, mine, :] = acc[:, j, mine, :] + r_lo[j]

            @pl.when(has_hi)
            def _():
                line_down(j).wait_recv()
                acc[:, j, mine, :] = acc[:, j, mine, :] + r_hi[j]

            for k in range(1, cols):
                across(j, k).start()

    def stage_across(j):
        @pl.when(z == root(j))
        def _():
            for k in range(1, cols):
                across(j, k).wait_recv()
            if cols <= 2:
                total = acc[:, j, mine, :]
                for k in range(1, cols):
                    total = total + r_y[k - 1, j]
            else:
                total = jnp.zeros((3, half, ch), F32)
                for i in range(cols):
                    term = acc[:, j, mine, :]
                    for k in range(1, cols):
                        term = jnp.where(lax.rem(y + cols - k, cols) == i, r_y[k - 1, j], term)
                    total = total + term
            fin[:, j, mine, :] = total * factor

            @pl.when(has_lo)
            def _():
                final_down(j).start()

            @pl.when(has_hi)
            def _():
                final_up(j).start()

            final_sibling(j).start()

    def stage_spread(j):
        @pl.when(z < root(j))
        def _():
            final_down(j).wait_recv()

            @pl.when(has_lo)
            def _():
                final_down(j).start()

            final_sibling(j).start()

        @pl.when(z > root(j))
        def _():
            final_up(j).wait_recv()

            @pl.when(has_hi)
            def _():
                final_up(j).start()

            final_sibling(j).start()

    def during(j, stage):
        @pl.when(jnp.logical_and(j >= 0, j < taps))
        def _():
            stage(j)

    lags = (
        (1, stage_sibling), (3, stage_line), (5, stage_root),
        (7, stage_across), (10, stage_spread),
    )
    steps = max(taps + 10, 2 * tiles)

    def step(s, carry):
        during(s, stage_send)

        @pl.when(s < tiles)
        def _():
            conv_tile(vp, wf, act, core, s, False)

        @pl.when(s == tiles)
        def _():
            await_off(1, grd, gp)

        @pl.when(jnp.logical_and(s >= tiles, s < 2 * tiles))
        def _():
            conv_tile(gp, wb, ing, core, s - tiles, True)

        for lag, stage in lags:
            during(s - lag, stage)
        return carry

    lax.fori_loop(0, steps, step, 0)

    act_copy = pltpu.make_async_copy(act, act_out, s_out.at[0])
    ing_copy = pltpu.make_async_copy(ing, ing_out, s_out.at[1])
    dw_copy = pltpu.make_async_copy(fin, dw_out, s_out.at[2])
    act_copy.start()
    ing_copy.start()

    def finish(j, carry):
        to_sibling(j).wait_send()
        final_sibling(j).wait_send()

        @pl.when(z != root(j))
        def _():
            line_up(j).wait_send()

        @pl.when(z == root(j))
        def _():
            for k in range(1, cols):
                across(j, k).wait_send()

        @pl.when(jnp.logical_and(has_lo, z <= root(j)))
        def _():
            final_down(j).wait_send()

        @pl.when(jnp.logical_and(has_hi, z >= root(j)))
        def _():
            final_up(j).wait_send()

        final_sibling(j).wait_recv()
        return carry

    lax.fori_loop(0, taps, finish, 0)
    dw_copy.start()

    for which, src, dst in ((0, vol, vp), (1, grd, gp)):
        halo_sibling(which, src, dst).wait_send()

        @pl.when(off_chip)
        def _(which=which, src=src, dst=dst):
            halo_off(which, src, dst).wait_send()

    act_copy.wait()
    ing_copy.wait()
    dw_copy.wait()


def results_kernel(act, ing, dw, act_out, ing_out, dw_out, sem):
    copies = []
    for src, dst in ((act, act_out), (ing, ing_out), (dw, dw_out)):
        for k in range(src.shape[0]):
            copies.append(pltpu.make_async_copy(src.at[k], dst.at[k], sem.at[len(copies)]))
    for copy in copies:
        copy.start()
    for copy in copies:
        copy.wait()


def body(n, line, cols, volume, kernel, grad_out):
    planes, height, breadth, ch = volume.shape
    cells = height * breadth
    half = ch // 2
    taps = 9
    tile = 8
    factor = float(np.float32(1.0) / np.sqrt(np.float32(n * planes * cells)))
    dma = pltpu.SemaphoreType.DMA
    peers = max(cols - 1, 1)
    flops = 3 * 2 * 27 * planes * cells * ch * ch
    outs = pl.pallas_call(
        functools.partial(layer_kernel, n, line, cols, height, breadth, ch, tile, factor),
        out_shape=(
            jax.ShapeDtypeStruct((planes, cells, ch), BF16),
            jax.ShapeDtypeStruct((planes, cells, ch), BF16),
            jax.ShapeDtypeStruct((3, taps, ch, ch), F32),
        ),
        in_specs=[pl.BlockSpec(memory_space=pl.ANY)] * 3,
        out_specs=[pl.BlockSpec(memory_space=pl.ANY)] * 3,
        scratch_shapes=[
            pltpu.VMEM((4, cells + 2 * breadth, ch), BF16),
            pltpu.VMEM((4, cells + 2 * breadth, ch), BF16),
            pltpu.VMEM((3, 3, ch, 3 * ch), BF16),
            pltpu.VMEM((3, 3, 3, ch, ch), BF16),
            pltpu.VMEM((9 * ch, 3 * ch), BF16),
            pltpu.VMEM((4 * ch, cells), BF16),
            pltpu.VMEM((3, 2, cells + 2 * breadth, ch), BF16),
            pltpu.VMEM((3, taps, ch, ch), F32),
            pltpu.VMEM((3, taps, ch, ch), F32),
            pltpu.VMEM((taps, 3, half, ch), F32),
            pltpu.VMEM((taps, 3, half, ch), F32),
            pltpu.VMEM((taps, 3, half, ch), F32),
            pltpu.VMEM((peers, taps, 3, half, ch), F32),
            pltpu.VMEM((planes, cells, ch), BF16),
            pltpu.VMEM((planes, cells, ch), BF16),
            dma((4,)), dma((4,)), dma((2, 2)), dma((2, 2)),
            dma((taps,)), dma((taps,)), dma((taps,)), dma((taps,)), dma((taps,)),
            dma((peers, taps)), dma((peers, taps)),
            dma((taps,)), dma((taps,)), dma((taps,)), dma((taps,)), dma((taps,)),
            dma((3,)),
        ],
        compiler_params=pltpu.CompilerParams(
            collective_id=0, has_side_effects=True, vmem_limit_bytes=56 * 1024 * 1024),
        cost_estimate=pl.CostEstimate(flops=flops, bytes_accessed=10_000_000, transcendentals=0),
    )(
        volume.reshape(planes, cells, ch),
        kernel,
        grad_out.reshape(planes, cells, ch),
    )
    outs = pl.pallas_call(
        results_kernel,
        out_shape=tuple(jax.ShapeDtypeStruct(o.shape, o.dtype) for o in outs),
        in_specs=[pl.BlockSpec(memory_space=pl.ANY)] * 3,
        out_specs=[pl.BlockSpec(memory_space=pl.ANY)] * 3,
        scratch_shapes=[dma((7,))],
        compiler_params=pltpu.CompilerParams(vmem_limit_bytes=56 * 1024 * 1024),
        cost_estimate=pl.CostEstimate(flops=0, bytes_accessed=8_000_000, transcendentals=0),
    )(*outs)
    activation = outs[0].reshape(volume.shape)
    input_grad = outs[1].reshape(volume.shape)
    return activation, input_grad, outs[2].reshape(3, 3, 3, ch, ch)


def solution(mesh):
    n = mesh.shape["slab"]
    chips = n // 2
    cols = 1
    while cols * cols * 4 <= chips:
        cols *= 2
    line = chips // cols
    return jax.shard_map(
        functools.partial(body, n, line, cols),
        mesh=mesh,
        in_specs=(
            P(("groups", "slab"), None, None, None),
            P(),
            P(("groups", "slab"), None, None, None),
        ),
        out_specs=(
            P(("groups", "slab"), None, None, None),
            P(("groups", "slab"), None, None, None),
            P("groups", None, None, None, None),
        ),
        check_vma=False,
    )
```

```python
import functools

import jax
import jax.numpy as jnp
import numpy as np
from jax import lax
from jax.experimental import pallas as pl
from jax.experimental.pallas import tpu as pltpu
from jax.sharding import PartitionSpec as P

MESH = pl.DeviceIdType.MESH
F32 = jnp.float32
BF16 = jnp.bfloat16


def layer_kernel(
    n, line, cols, height, breadth, ch, tile, factor,
    vol, ker, grd,
    act_out, ing_out, dw_out,
    vp, gp, wf, wk, wb, xt, gs, acc, fin, r_sib, r_lo, r_hi, r_y, act, ing,
    s_in, s_w, s_hs, s_hr, s_sib, r_sibs, s_line, r_los, r_his, s_y, r_ys,
    s_up, s_dn, s_fs, r_fin, r_fsib, s_out,
):
    cells = height * breadth
    half = ch // 2
    taps = 9
    me = lax.axis_index("slab")
    core = lax.rem(me, 2)
    chip = me // 2
    z = chip // cols
    y = lax.rem(chip, cols)
    sib = me + 1 - 2 * core
    zlo = me - 2 * cols
    zhi = me + 2 * cols
    has_lo, has_hi = z > 0, z < line - 1
    has_before, has_after = me > 0, me < n - 1

    def peer(k):
        return (z * cols + lax.rem(y + k, cols)) * 2 + core

    inner = pl.ds(breadth, cells)
    loads = []
    for p in range(2):
        loads.append(pltpu.make_async_copy(vol.at[p], vp.at[p + 1, inner], s_in.at[p]))
    for p in range(2):
        loads.append(pltpu.make_async_copy(grd.at[p], gp.at[p + 1, inner], s_in.at[p + 2]))
    for copy in loads:
        copy.start()
    wloads = []
    for c in range(3):
        wloads.append(pltpu.make_async_copy(
            ker.at[:, :, c], wf.at[:, :, :, pl.ds(c * ch, ch)], s_w.at[c]))
    wloads.append(pltpu.make_async_copy(ker, wk, s_w.at[3]))
    for copy in wloads:
        copy.start()

    barrier = pltpu.get_barrier_semaphore()

    def greet(dev):
        pl.semaphore_signal(barrier, inc=1, device_id={"slab": dev}, device_id_type=MESH)

    for k in range(1, cols):
        greet(peer(k))
    for cond, dev in ((has_before, me - 1), (has_after, me + 1), (has_lo, zlo), (has_hi, zhi)):
        @pl.when(cond)
        def _(dev=dev):
            greet(dev)
    partners = cols - 1
    for cond in (has_before, has_after, has_lo, has_hi):
        partners = partners + cond.astype(jnp.int32)
    pl.semaphore_wait(barrier, partners)

    def remote(src, dst, ssem, rsem, dev):
        return pltpu.make_async_remote_copy(
            src_ref=src, dst_ref=dst, send_sem=ssem, recv_sem=rsem,
            device_id={"slab": dev}, device_id_type=MESH)

    off_chip = jnp.where(core == 0, has_before, has_after)
    off_dev = me - 1 + 2 * core
    inside = 1 - core
    slot_sib, slot_off = 3 * inside, 3 * core

    def halo_sibling(which, src, dst):
        return remote(src.at[inside], dst.at[3 * core, inner], s_hs.at[which, 0], s_hr.at[which, 0], sib)

    def halo_off(which, src, dst):
        return remote(src.at[core], dst.at[3 * inside, inner], s_hs.at[which, 1], s_hr.at[which, 1], off_dev)

    def await_sibling(which, src, dst):
        remote(src.at[inside], dst.at[slot_sib, inner], s_hs.at[which, 0], s_hr.at[which, 0], sib).wait_recv()

    def await_off(which, src, dst):
        @pl.when(off_chip)
        def _():
            remote(src.at[core], dst.at[slot_off, inner], s_hs.at[which, 1], s_hr.at[which, 1], off_dev).wait_recv()

    @pl.when(off_chip)
    def _():
        halo_off(0, vol, vp).start()

    halo_sibling(0, vol, vp).start()
    halo_sibling(1, grd, gp).start()

    edge = jnp.zeros((breadth, ch), BF16)
    for ref in (vp, gp):
        for p in range(4):
            ref[p, pl.ds(0, breadth), :] = edge
            ref[p, pl.ds(breadth + cells, breadth), :] = edge
    for c in range(3):
        for d in range(2):
            gs[c, d, pl.ds(0, breadth), :] = edge
            gs[c, d, pl.ds(breadth + cells, breadth), :] = edge
    for cond, p in ((me == 0, 0), (me == n - 1, 3)):
        @pl.when(cond)
        def _(p=p):
            vp[p, inner, :] = jnp.zeros((cells, ch), BF16)
            gp[p, inner, :] = jnp.zeros((cells, ch), BF16)

    rows = tile * breadth
    tiles = height // tile
    column = lax.rem(lax.broadcasted_iota(jnp.int32, (rows, ch), 0), breadth)

    def before_of(v):
        return jnp.where(column == 0, 0.0, pltpu.roll(v, 1, 0))

    def after_of(v):
        return jnp.where(column == breadth - 1, 0.0, pltpu.roll(v, rows - 1, 0))

    for copy in loads:
        copy.wait()

    def shift_tile(k, carry):
        at = pl.ds(pl.multiple_of(breadth + k * rows, 16), rows)
        for d in range(2):
            plane = gp[d + 1, at, :]
            wide = plane.astype(F32)
            gs[0, d, at, :] = after_of(wide).astype(BF16)
            gs[1, d, at, :] = plane
            gs[2, d, at, :] = before_of(wide).astype(BF16)
        return carry

    lax.fori_loop(0, tiles, shift_tile, 0)

    def transpose_planes(pairs):
        def one(j, carry):
            at = pl.ds(pl.multiple_of(breadth + j * ch, 16), ch)
            to = pl.ds(pl.multiple_of(j * ch, ch), ch)
            for p, row in pairs:
                xt[pl.ds(row * ch, ch), to] = vp[p, at, :].T
            return carry
        lax.fori_loop(0, cells // ch, one, 0)

    def grads(t, d):
        b, c = t // 3, lax.rem(t, 3)
        return gs[c, d, pl.ds(pl.multiple_of((2 - b) * breadth, 16), cells), :]

    await_sibling(0, vol, vp)
    transpose_planes(((1, 0), (2, 1), (slot_sib, 2)))

    def own_part(t):
        rhs = jnp.concatenate([grads(t, 0), grads(t, 1)], axis=1)
        full = jnp.dot(xt[pl.ds(0, 3 * ch), :], rhs, preferred_element_type=F32)
        beside = full[2 * ch:]
        acc[t] = full[:ch, ch:] + jnp.where(core == 1, beside[:, :ch], 0.0)
        acc[taps + t] = full[:ch, :ch] + full[ch:2 * ch, ch:]
        acc[2 * taps + t] = full[ch:2 * ch, :ch] + jnp.where(core == 0, beside[:, ch:], 0.0)

    def conv_tile(planes, weights, out, d, k, backward):
        start = k * rows
        bands = []
        for a in range(3):
            for b in range(3):
                at = pl.ds(pl.multiple_of(start + b * breadth, 16), rows)
                bands.append(planes[d + a, at, :])
        lhs = jnp.concatenate(bands, axis=1)
        if backward:
            rhs = weights[...]
        else:
            rhs = jnp.concatenate([weights[a, b] for a in range(3) for b in range(3)], axis=0)
        sums = jnp.dot(lhs, rhs, preferred_element_type=F32)
        first, last = sums[:, :ch], sums[:, 2 * ch:]
        total = sums[:, ch:2 * ch] + before_of(first) + after_of(last)
        out[d, pl.ds(pl.multiple_of(start, 16), rows), :] = total.astype(BF16)

    mine = pl.ds(pl.multiple_of(core * half, half), half)
    other = pl.ds(pl.multiple_of((1 - core) * half, half), half)

    def root(j):
        return (line - 1) // 2 + lax.rem(j, 2) * (line // 2 - (line - 1) // 2)

    def spot(j):
        return lax.rem(j + taps, 3 * taps)

    def to_sibling(j):
        return remote(acc.at[spot(j), other], r_sib.at[j], s_sib.at[j], r_sibs.at[j], sib)

    def line_up(j):
        return remote(acc.at[spot(j), mine], r_lo.at[j], s_line.at[j], r_los.at[j], zhi)

    def line_down(j):
        return remote(acc.at[spot(j), mine], r_hi.at[j], s_line.at[j], r_his.at[j], zlo)

    def across(j, k):
        return remote(acc.at[spot(j), mine], r_y.at[k - 1, j], s_y.at[k - 1, j], r_ys.at[k - 1, j], peer(k))

    def final_up(j):
        return remote(fin.at[spot(j), mine], fin.at[spot(j), mine], s_up.at[j], r_fin.at[j], zhi)

    def final_down(j):
        return remote(fin.at[spot(j), mine], fin.at[spot(j), mine], s_dn.at[j], r_fin.at[j], zlo)

    def final_sibling(j):
        return remote(fin.at[spot(j), mine], fin.at[spot(j), mine], s_fs.at[j], r_fsib.at[j], sib)

    def stage_send(j):
        @pl.when(j < taps)
        def _():
            own_part(j)

        @pl.when(jnp.logical_or(
            jnp.logical_and(core == 1, jnp.logical_and(j >= taps, j < 2 * taps)),
            jnp.logical_and(core == 0, j >= 2 * taps)))
        def _():
            part = jnp.dot(
                xt[pl.ds(3 * ch, ch), :], grads(lax.rem(j, taps), core), preferred_element_type=F32)
            acc[spot(j)] = acc[spot(j)] + part

        to_sibling(j).start()

    def stage_sibling(j):
        to_sibling(j).wait_recv()
        acc[spot(j), mine, :] = acc[spot(j), mine, :] + r_sib[j]

        @pl.when(jnp.logical_and(z == 0, root(j) != 0))
        def _():
            line_up(j).start()

        @pl.when(jnp.logical_and(z == line - 1, root(j) != line - 1))
        def _():
            line_down(j).start()

    def stage_line(j):
        @pl.when(jnp.logical_and(z > 0, z < root(j)))
        def _():
            line_up(j).wait_recv()
            acc[spot(j), mine, :] = acc[spot(j), mine, :] + r_lo[j]
            line_up(j).start()

        @pl.when(jnp.logical_and(z < line - 1, z > root(j)))
        def _():
            line_down(j).wait_recv()
            acc[spot(j), mine, :] = acc[spot(j), mine, :] + r_hi[j]
            line_down(j).start()

    def stage_root(j):
        @pl.when(z == root(j))
        def _():
            @pl.when(has_lo)
            def _():
                line_up(j).wait_recv()
                acc[spot(j), mine, :] = acc[spot(j), mine, :] + r_lo[j]

            @pl.when(has_hi)
            def _():
                line_down(j).wait_recv()
                acc[spot(j), mine, :] = acc[spot(j), mine, :] + r_hi[j]

            for k in range(1, cols):
                across(j, k).start()

    def stage_across(j):
        @pl.when(z == root(j))
        def _():
            for k in range(1, cols):
                across(j, k).wait_recv()
            if cols <= 2:
                total = acc[spot(j), mine, :]
                for k in range(1, cols):
                    total = total + r_y[k - 1, j]
            else:
                total = jnp.zeros((half, ch), F32)
                for i in range(cols):
                    term = acc[spot(j), mine, :]
                    for k in range(1, cols):
                        term = jnp.where(lax.rem(y + cols - k, cols) == i, r_y[k - 1, j], term)
                    total = total + term
            fin[spot(j), mine, :] = total * factor

            @pl.when(has_lo)
            def _():
                final_down(j).start()

            @pl.when(has_hi)
            def _():
                final_up(j).start()

            final_sibling(j).start()

    def stage_spread(j):
        @pl.when(z < root(j))
        def _():
            final_down(j).wait_recv()

            @pl.when(has_lo)
            def _():
                final_down(j).start()

            final_sibling(j).start()

        @pl.when(z > root(j))
        def _():
            final_up(j).wait_recv()

            @pl.when(has_hi)
            def _():
                final_up(j).start()

            final_sibling(j).start()

    begin_act, begin_ing, begin_halo = taps, taps + tiles, taps + 2 * tiles
    end_halo = begin_halo + 2 * taps
    gap = begin_halo - taps

    def during(at, stage):
        first = jnp.logical_and(at >= 0, at < taps)
        second = jnp.logical_and(at >= begin_halo, at < end_halo)

        @pl.when(jnp.logical_or(first, second))
        def _():
            stage(at - gap * (at >= begin_halo).astype(jnp.int32))

    def spread_near(j):
        @pl.when(jnp.logical_and(z >= root(j) - 1, z <= root(j) + 1))
        def _():
            stage_spread(j)

    def spread_far(j):
        @pl.when(jnp.logical_or(z < root(j) - 1, z > root(j) + 1))
        def _():
            stage_spread(j)

    lags = (
        (2, stage_sibling), (5, stage_line), (8, stage_root),
        (11, stage_across), (14, spread_near), (17, spread_far),
    )
    steps = end_halo + 17

    def step(s, carry):
        late = (s >= begin_halo).astype(jnp.int32)
        plane = inside + late * (core - inside)

        @pl.when(s == begin_halo)
        def _():
            await_off(0, vol, vp)

            @pl.when(off_chip)
            def _():
                halo_off(1, grd, gp).start()

            transpose_planes(((slot_off, 3),))

        during(s, stage_send)

        @pl.when(s == begin_act)
        def _():
            for copy in wloads:
                copy.wait()

        @pl.when(jnp.logical_or(
            jnp.logical_and(s >= begin_act, s < begin_ing),
            jnp.logical_and(s >= begin_halo, s < begin_halo + tiles)))
        def _():
            conv_tile(vp, wf, act, plane, s - begin_act - late * (begin_halo - begin_act), False)

        @pl.when(s == begin_ing)
        def _():
            for a in range(3):
                for b in range(3):
                    for c in range(3):
                        wb[pl.ds((3 * a + b) * ch, ch), pl.ds(c * ch, ch)] = wk[2 - a, 2 - b, 2 - c].T
            await_sibling(1, grd, gp)

        @pl.when(s == end_halo)
        def _():
            await_off(1, grd, gp)

        @pl.when(jnp.logical_or(
            jnp.logical_and(s >= begin_ing, s < begin_halo),
            jnp.logical_and(s >= end_halo, s < end_halo + tiles)))
        def _():
            conv_tile(gp, wb, ing, plane, s - begin_ing - late * (end_halo - begin_ing), True)

        for lag, stage in lags:
            during(s - lag, stage)
        return carry

    lax.fori_loop(0, steps, step, 0)

    act_copy = pltpu.make_async_copy(act, act_out, s_out.at[0])
    ing_copy = pltpu.make_async_copy(ing, ing_out, s_out.at[1])
    dw_copy = pltpu.make_async_copy(fin, dw_out, s_out.at[2])
    act_copy.start()
    ing_copy.start()

    def finish(j, carry):
        to_sibling(j).wait_send()
        final_sibling(j).wait_send()

        @pl.when(z != root(j))
        def _():
            line_up(j).wait_send()

        @pl.when(z == root(j))
        def _():
            for k in range(1, cols):
                across(j, k).wait_send()

        @pl.when(jnp.logical_and(has_lo, z <= root(j)))
        def _():
            final_down(j).wait_send()

        @pl.when(jnp.logical_and(has_hi, z >= root(j)))
        def _():
            final_up(j).wait_send()

        final_sibling(j).wait_recv()
        return carry

    lax.fori_loop(0, 3 * taps, finish, 0)
    dw_copy.start()

    for which, src, dst in ((0, vol, vp), (1, grd, gp)):
        halo_sibling(which, src, dst).wait_send()

        @pl.when(off_chip)
        def _(which=which, src=src, dst=dst):
            halo_off(which, src, dst).wait_send()

    act_copy.wait()
    ing_copy.wait()
    dw_copy.wait()


def results_kernel(act, ing, dw, act_out, ing_out, dw_out):
    act_out[...] = act[...]
    ing_out[...] = ing[...]
    dw_out[...] = dw[...]


def body(n, line, cols, volume, kernel, grad_out):
    planes, height, breadth, ch = volume.shape
    cells = height * breadth
    half = ch // 2
    chunks = 27
    tile = 8
    factor = float(np.float32(1.0) / np.sqrt(np.float32(n * planes * cells)))
    dma = pltpu.SemaphoreType.DMA
    peers = max(cols - 1, 1)
    flops = 3 * 2 * 27 * planes * cells * ch * ch
    outs = pl.pallas_call(
        functools.partial(layer_kernel, n, line, cols, height, breadth, ch, tile, factor),
        out_shape=(
            jax.ShapeDtypeStruct((planes, cells, ch), BF16),
            jax.ShapeDtypeStruct((planes, cells, ch), BF16),
            jax.ShapeDtypeStruct((chunks, ch, ch), F32),
        ),
        in_specs=[pl.BlockSpec(memory_space=pl.ANY)] * 3,
        out_specs=[pl.BlockSpec(memory_space=pl.ANY)] * 3,
        scratch_shapes=[
            pltpu.VMEM((4, cells + 2 * breadth, ch), BF16),
            pltpu.VMEM((4, cells + 2 * breadth, ch), BF16),
            pltpu.VMEM((3, 3, ch, 3 * ch), BF16),
            pltpu.VMEM((3, 3, 3, ch, ch), BF16),
            pltpu.VMEM((9 * ch, 3 * ch), BF16),
            pltpu.VMEM((4 * ch, cells), BF16),
            pltpu.VMEM((3, 2, cells + 2 * breadth, ch), BF16),
            pltpu.VMEM((chunks, ch, ch), F32),
            pltpu.VMEM((chunks, ch, ch), F32),
            pltpu.VMEM((chunks, half, ch), F32),
            pltpu.VMEM((chunks, half, ch), F32),
            pltpu.VMEM((chunks, half, ch), F32),
            pltpu.VMEM((peers, chunks, half, ch), F32),
            pltpu.VMEM((planes, cells, ch), BF16),
            pltpu.VMEM((planes, cells, ch), BF16),
            dma((4,)), dma((4,)), dma((2, 2)), dma((2, 2)),
            dma((chunks,)), dma((chunks,)), dma((chunks,)), dma((chunks,)), dma((chunks,)),
            dma((peers, chunks)), dma((peers, chunks)),
            dma((chunks,)), dma((chunks,)), dma((chunks,)), dma((chunks,)), dma((chunks,)),
            dma((3,)),
        ],
        compiler_params=pltpu.CompilerParams(
            collective_id=0, has_side_effects=True, vmem_limit_bytes=56 * 1024 * 1024),
        cost_estimate=pl.CostEstimate(flops=flops, bytes_accessed=10_000_000, transcendentals=0),
    )(
        volume.reshape(planes, cells, ch),
        kernel,
        grad_out.reshape(planes, cells, ch),
    )
    parts = 6
    pieces = [
        outs[0].reshape(parts, -1, ch), outs[1].reshape(parts, -1, ch), outs[2].reshape(parts, -1, ch)]
    blocks = [pl.BlockSpec((1, piece.shape[1], ch), lambda i: (i, 0, 0)) for piece in pieces]
    outs = pl.pallas_call(
        results_kernel,
        grid=(parts,),
        out_shape=[jax.ShapeDtypeStruct(piece.shape, piece.dtype) for piece in pieces],
        in_specs=blocks,
        out_specs=blocks,
        compiler_params=pltpu.CompilerParams(vmem_limit_bytes=56 * 1024 * 1024),
        cost_estimate=pl.CostEstimate(flops=0, bytes_accessed=8_000_000, transcendentals=0),
    )(*pieces)
    activation = outs[0].reshape(volume.shape)
    input_grad = outs[1].reshape(volume.shape)
    return activation, input_grad, outs[2].reshape(3, 3, 3, ch, ch)


def solution(mesh):
    n = mesh.shape["slab"]
    chips = n // 2
    cols = 1
    while cols * cols * 4 <= chips:
        cols *= 2
    line = chips // cols
    return jax.shard_map(
        functools.partial(body, n, line, cols),
        mesh=mesh,
        in_specs=(
            P(("groups", "slab"), None, None, None),
            P(),
            P(("groups", "slab"), None, None, None),
        ),
        out_specs=(
            P(("groups", "slab"), None, None, None),
            P(("groups", "slab"), None, None, None),
            P("groups", None, None, None, None),
        ),
        check_vma=False,
    )
```

```python
import functools

import jax
import jax.numpy as jnp
import numpy as np
from jax import lax
from jax.experimental import pallas as pl
from jax.experimental.pallas import tpu as pltpu
from jax.sharding import PartitionSpec as P

MESH = pl.DeviceIdType.MESH
F32 = jnp.float32
BF16 = jnp.bfloat16


def layer_kernel(
    n, line, cols, height, breadth, ch, tile, factor,
    vol, ker, grd,
    act_out, ing_out, dw_out,
    vp, gp, wf, wk, wb, xt, gs, acc, fin, r_sib, r_lo, r_hi, r_y, act, ing,
    s_in, s_w, s_hs, s_hr, s_sib, r_sibs, s_line, r_los, r_his, s_y, r_ys,
    s_up, s_dn, s_fs, r_fin, r_fsib, s_out,
):
    cells = height * breadth
    half = ch // 2
    taps = 9
    me = lax.axis_index("slab")
    core = lax.rem(me, 2)
    chip = me // 2
    z = chip // cols
    y = lax.rem(chip, cols)
    sib = me + 1 - 2 * core
    zlo = me - 2 * cols
    zhi = me + 2 * cols
    has_lo, has_hi = z > 0, z < line - 1
    has_before, has_after = me > 0, me < n - 1

    def peer(k):
        return (z * cols + lax.rem(y + k, cols)) * 2 + core

    inner = pl.ds(breadth, cells)
    loads = []
    for p in range(2):
        loads.append(pltpu.make_async_copy(vol.at[p], vp.at[p + 1, inner], s_in.at[p]))
    for p in range(2):
        loads.append(pltpu.make_async_copy(grd.at[p], gp.at[p + 1, inner], s_in.at[p + 2]))
    for copy in loads:
        copy.start()
    wloads = []
    for c in range(3):
        wloads.append(pltpu.make_async_copy(
            ker.at[:, :, c], wf.at[:, :, :, pl.ds(c * ch, ch)], s_w.at[c]))
    wloads.append(pltpu.make_async_copy(ker, wk, s_w.at[3]))
    for copy in wloads:
        copy.start()

    barrier = pltpu.get_barrier_semaphore()

    def greet(dev):
        pl.semaphore_signal(barrier, inc=1, device_id={"slab": dev}, device_id_type=MESH)

    for k in range(1, cols):
        greet(peer(k))
    for cond, dev in ((has_before, me - 1), (has_after, me + 1), (has_lo, zlo), (has_hi, zhi)):
        @pl.when(cond)
        def _(dev=dev):
            greet(dev)
    partners = cols - 1
    for cond in (has_before, has_after, has_lo, has_hi):
        partners = partners + cond.astype(jnp.int32)
    pl.semaphore_wait(barrier, partners)

    def remote(src, dst, ssem, rsem, dev):
        return pltpu.make_async_remote_copy(
            src_ref=src, dst_ref=dst, send_sem=ssem, recv_sem=rsem,
            device_id={"slab": dev}, device_id_type=MESH)

    off_chip = jnp.where(core == 0, has_before, has_after)
    off_dev = me - 1 + 2 * core
    inside = 1 - core
    slot_sib, slot_off = 3 * inside, 3 * core

    def halo_sibling(which, dst):
        return remote(dst.at[1 + inside, inner], dst.at[3 * core, inner], s_hs.at[which, 0], s_hr.at[which, 0], sib)

    def halo_off(which, dst):
        return remote(dst.at[1 + core, inner], dst.at[3 * inside, inner], s_hs.at[which, 1], s_hr.at[which, 1], off_dev)

    def await_sibling(which, dst):
        remote(dst.at[1 + inside, inner], dst.at[slot_sib, inner], s_hs.at[which, 0], s_hr.at[which, 0], sib).wait_recv()

    def await_off(which, dst):
        @pl.when(off_chip)
        def _():
            remote(dst.at[1 + core, inner], dst.at[slot_off, inner], s_hs.at[which, 1], s_hr.at[which, 1], off_dev).wait_recv()

    for copy in loads[:2]:
        copy.wait()

    @pl.when(off_chip)
    def _():
        halo_off(0, vp).start()

    halo_sibling(0, vp).start()
    for copy in loads[2:]:
        copy.wait()
    halo_sibling(1, gp).start()

    edge = jnp.zeros((breadth, ch), BF16)
    for ref in (vp, gp):
        for p in range(4):
            ref[p, pl.ds(0, breadth), :] = edge
            ref[p, pl.ds(breadth + cells, breadth), :] = edge
    for c in range(3):
        for d in range(2):
            gs[c, d, pl.ds(0, breadth), :] = edge
            gs[c, d, pl.ds(breadth + cells, breadth), :] = edge
    for cond, p in ((me == 0, 0), (me == n - 1, 3)):
        @pl.when(cond)
        def _(p=p):
            vp[p, inner, :] = jnp.zeros((cells, ch), BF16)
            gp[p, inner, :] = jnp.zeros((cells, ch), BF16)

    rows = tile * breadth
    tiles = height // tile
    column = lax.rem(lax.broadcasted_iota(jnp.int32, (rows, ch), 0), breadth)

    def before_of(v):
        return jnp.where(column == 0, 0.0, pltpu.roll(v, 1, 0))

    def after_of(v):
        return jnp.where(column == breadth - 1, 0.0, pltpu.roll(v, rows - 1, 0))

    def shift_tile(k, carry):
        at = pl.ds(pl.multiple_of(breadth + k * rows, 16), rows)
        for d in range(2):
            plane = gp[d + 1, at, :]
            wide = plane.astype(F32)
            gs[0, d, at, :] = after_of(wide).astype(BF16)
            gs[1, d, at, :] = plane
            gs[2, d, at, :] = before_of(wide).astype(BF16)
        return carry

    lax.fori_loop(0, tiles, shift_tile, 0)

    def transpose_planes(pairs):
        def one(j, carry):
            at = pl.ds(pl.multiple_of(breadth + j * ch, 16), ch)
            to = pl.ds(pl.multiple_of(j * ch, ch), ch)
            for p, row in pairs:
                xt[pl.ds(row * ch, ch), to] = vp[p, at, :].T
            return carry
        lax.fori_loop(0, cells // ch, one, 0)

    def grads(t, d):
        b, c = t // 3, lax.rem(t, 3)
        return gs[c, d, pl.ds(pl.multiple_of((2 - b) * breadth, 16), cells), :]

    await_sibling(0, vp)
    transpose_planes(((1, 0), (2, 1), (slot_sib, 2)))

    def own_part(t):
        rhs = jnp.concatenate([grads(t, 0), grads(t, 1)], axis=1)
        full = jnp.dot(xt[pl.ds(0, 3 * ch), :], rhs, preferred_element_type=F32)
        beside = full[2 * ch:]
        acc[t] = full[:ch, ch:] + jnp.where(core == 1, beside[:, :ch], 0.0)
        acc[taps + t] = full[:ch, :ch] + full[ch:2 * ch, ch:]
        acc[2 * taps + t] = full[ch:2 * ch, :ch] + jnp.where(core == 0, beside[:, ch:], 0.0)

    def conv_tile(planes, weights, out, d, k, backward):
        start = k * rows
        bands = []
        for a in range(3):
            for b in range(3):
                at = pl.ds(pl.multiple_of(start + b * breadth, 16), rows)
                bands.append(planes[d + a, at, :])
        lhs = jnp.concatenate(bands, axis=1)
        if backward:
            rhs = weights[...]
        else:
            rhs = jnp.concatenate([weights[a, b] for a in range(3) for b in range(3)], axis=0)
        sums = jnp.dot(lhs, rhs, preferred_element_type=F32)
        first, last = sums[:, :ch], sums[:, 2 * ch:]
        total = sums[:, ch:2 * ch] + before_of(first) + after_of(last)
        out[d, pl.ds(pl.multiple_of(start, 16), rows), :] = total.astype(BF16)

    mine = pl.ds(pl.multiple_of(core * half, half), half)
    other = pl.ds(pl.multiple_of((1 - core) * half, half), half)

    def root(j):
        return (line - 1) // 2 + lax.rem(j, 2) * (line // 2 - (line - 1) // 2)

    def spot(j):
        return lax.rem(j + taps, 3 * taps)

    def to_sibling(j):
        return remote(acc.at[spot(j), other], r_sib.at[j], s_sib.at[j], r_sibs.at[j], sib)

    def line_up(j):
        return remote(acc.at[spot(j), mine], r_lo.at[j], s_line.at[j], r_los.at[j], zhi)

    def line_down(j):
        return remote(acc.at[spot(j), mine], r_hi.at[j], s_line.at[j], r_his.at[j], zlo)

    def across(j, k):
        return remote(acc.at[spot(j), mine], r_y.at[k - 1, j], s_y.at[k - 1, j], r_ys.at[k - 1, j], peer(k))

    def final_up(j):
        return remote(fin.at[spot(j), mine], fin.at[spot(j), mine], s_up.at[j], r_fin.at[j], zhi)

    def final_down(j):
        return remote(fin.at[spot(j), mine], fin.at[spot(j), mine], s_dn.at[j], r_fin.at[j], zlo)

    def final_sibling(j):
        return remote(fin.at[spot(j), mine], fin.at[spot(j), mine], s_fs.at[j], r_fsib.at[j], sib)

    def stage_send(j):
        @pl.when(j < taps)
        def _():
            own_part(j)

        @pl.when(jnp.logical_or(
            jnp.logical_and(core == 1, jnp.logical_and(j >= taps, j < 2 * taps)),
            jnp.logical_and(core == 0, j >= 2 * taps)))
        def _():
            part = jnp.dot(
                xt[pl.ds(3 * ch, ch), :], grads(lax.rem(j, taps), core), preferred_element_type=F32)
            acc[spot(j)] = acc[spot(j)] + part

        to_sibling(j).start()

    def stage_sibling(j):
        to_sibling(j).wait_recv()
        acc[spot(j), mine, :] = acc[spot(j), mine, :] + r_sib[j]

        @pl.when(jnp.logical_and(z == 0, root(j) != 0))
        def _():
            line_up(j).start()

        @pl.when(jnp.logical_and(z == line - 1, root(j) != line - 1))
        def _():
            line_down(j).start()

    def stage_line(j):
        @pl.when(jnp.logical_and(z > 0, z < root(j)))
        def _():
            line_up(j).wait_recv()
            acc[spot(j), mine, :] = acc[spot(j), mine, :] + r_lo[j]
            line_up(j).start()

        @pl.when(jnp.logical_and(z < line - 1, z > root(j)))
        def _():
            line_down(j).wait_recv()
            acc[spot(j), mine, :] = acc[spot(j), mine, :] + r_hi[j]
            line_down(j).start()

    def stage_root(j):
        @pl.when(z == root(j))
        def _():
            @pl.when(has_lo)
            def _():
                line_up(j).wait_recv()
                acc[spot(j), mine, :] = acc[spot(j), mine, :] + r_lo[j]

            @pl.when(has_hi)
            def _():
                line_down(j).wait_recv()
                acc[spot(j), mine, :] = acc[spot(j), mine, :] + r_hi[j]

            for k in range(1, cols):
                across(j, k).start()

    def stage_across(j):
        @pl.when(z == root(j))
        def _():
            for k in range(1, cols):
                across(j, k).wait_recv()
            if cols <= 2:
                total = acc[spot(j), mine, :]
                for k in range(1, cols):
                    total = total + r_y[k - 1, j]
            else:
                total = jnp.zeros((half, ch), F32)
                for i in range(cols):
                    term = acc[spot(j), mine, :]
                    for k in range(1, cols):
                        term = jnp.where(lax.rem(y + cols - k, cols) == i, r_y[k - 1, j], term)
                    total = total + term
            fin[spot(j), mine, :] = total * factor

            @pl.when(has_lo)
            def _():
                final_down(j).start()

            @pl.when(has_hi)
            def _():
                final_up(j).start()

            final_sibling(j).start()

    def stage_spread(j):
        @pl.when(z < root(j))
        def _():
            final_down(j).wait_recv()

            @pl.when(has_lo)
            def _():
                final_down(j).start()

            final_sibling(j).start()

        @pl.when(z > root(j))
        def _():
            final_up(j).wait_recv()

            @pl.when(has_hi)
            def _():
                final_up(j).start()

            final_sibling(j).start()

    begin_act, begin_ing, begin_halo = taps, taps + tiles, taps + 2 * tiles
    end_halo = begin_halo + 2 * taps
    gap = begin_halo - taps

    def during(at, stage):
        first = jnp.logical_and(at >= 0, at < taps)
        second = jnp.logical_and(at >= begin_halo, at < end_halo)

        @pl.when(jnp.logical_or(first, second))
        def _():
            stage(at - gap * (at >= begin_halo).astype(jnp.int32))

    def spread_near(j):
        @pl.when(jnp.logical_and(z >= root(j) - 1, z <= root(j) + 1))
        def _():
            stage_spread(j)

    def spread_far(j):
        @pl.when(jnp.logical_or(z < root(j) - 1, z > root(j) + 1))
        def _():
            stage_spread(j)

    lags = (
        (2, stage_sibling), (5, stage_line), (8, stage_root),
        (11, stage_across), (14, spread_near), (17, spread_far),
    )
    steps = end_halo + 17

    def step(s, carry):
        late = (s >= begin_halo).astype(jnp.int32)
        plane = inside + late * (core - inside)

        @pl.when(s == begin_halo)
        def _():
            await_off(0, vp)

            @pl.when(off_chip)
            def _():
                halo_off(1, gp).start()

            transpose_planes(((slot_off, 3),))

        during(s, stage_send)

        @pl.when(s == begin_act)
        def _():
            for copy in wloads:
                copy.wait()

        @pl.when(jnp.logical_or(
            jnp.logical_and(s >= begin_act, s < begin_ing),
            jnp.logical_and(s >= begin_halo, s < begin_halo + tiles)))
        def _():
            conv_tile(vp, wf, act, plane, s - begin_act - late * (begin_halo - begin_act), False)

        @pl.when(s == begin_ing)
        def _():
            for a in range(3):
                for b in range(3):
                    for c in range(3):
                        wb[pl.ds((3 * a + b) * ch, ch), pl.ds(c * ch, ch)] = wk[2 - a, 2 - b, 2 - c].T
            await_sibling(1, gp)

        @pl.when(s == end_halo)
        def _():
            await_off(1, gp)

        @pl.when(jnp.logical_or(
            jnp.logical_and(s >= begin_ing, s < begin_halo),
            jnp.logical_and(s >= end_halo, s < end_halo + tiles)))
        def _():
            conv_tile(gp, wb, ing, plane, s - begin_ing - late * (end_halo - begin_ing), True)

        for lag, stage in lags:
            during(s - lag, stage)
        return carry

    lax.fori_loop(0, steps, step, 0)

    act_copy = pltpu.make_async_copy(act, act_out, s_out.at[0])
    ing_copy = pltpu.make_async_copy(ing, ing_out, s_out.at[1])
    dw_copy = pltpu.make_async_copy(fin, dw_out, s_out.at[2])
    act_copy.start()
    ing_copy.start()

    def finish(j, carry):
        to_sibling(j).wait_send()
        final_sibling(j).wait_send()

        @pl.when(z != root(j))
        def _():
            line_up(j).wait_send()

        @pl.when(z == root(j))
        def _():
            for k in range(1, cols):
                across(j, k).wait_send()

        @pl.when(jnp.logical_and(has_lo, z <= root(j)))
        def _():
            final_down(j).wait_send()

        @pl.when(jnp.logical_and(has_hi, z >= root(j)))
        def _():
            final_up(j).wait_send()

        final_sibling(j).wait_recv()
        return carry

    lax.fori_loop(0, 3 * taps, finish, 0)
    dw_copy.start()

    for which, dst in ((0, vp), (1, gp)):
        halo_sibling(which, dst).wait_send()

        @pl.when(off_chip)
        def _(which=which, dst=dst):
            halo_off(which, dst).wait_send()

    act_copy.wait()
    ing_copy.wait()
    dw_copy.wait()


def body(n, line, cols, volume, kernel, grad_out):
    planes, height, breadth, ch = volume.shape
    cells = height * breadth
    half = ch // 2
    chunks = 27
    tile = 8
    factor = float(np.float32(1.0) / np.sqrt(np.float32(n * planes * cells)))
    dma = pltpu.SemaphoreType.DMA
    peers = max(cols - 1, 1)
    flops = 3 * 2 * 27 * planes * cells * ch * ch
    outs = pl.pallas_call(
        functools.partial(layer_kernel, n, line, cols, height, breadth, ch, tile, factor),
        out_shape=(
            jax.ShapeDtypeStruct((planes, cells, ch), BF16),
            jax.ShapeDtypeStruct((planes, cells, ch), BF16),
            jax.ShapeDtypeStruct((chunks, ch, ch), F32),
        ),
        in_specs=[pl.BlockSpec(memory_space=pl.ANY)] * 3,
        out_specs=[pl.BlockSpec(memory_space=pl.ANY)] * 3,
        scratch_shapes=[
            pltpu.VMEM((4, cells + 2 * breadth, ch), BF16),
            pltpu.VMEM((4, cells + 2 * breadth, ch), BF16),
            pltpu.VMEM((3, 3, ch, 3 * ch), BF16),
            pltpu.VMEM((3, 3, 3, ch, ch), BF16),
            pltpu.VMEM((9 * ch, 3 * ch), BF16),
            pltpu.VMEM((4 * ch, cells), BF16),
            pltpu.VMEM((3, 2, cells + 2 * breadth, ch), BF16),
            pltpu.VMEM((chunks, ch, ch), F32),
            pltpu.VMEM((chunks, ch, ch), F32),
            pltpu.VMEM((chunks, half, ch), F32),
            pltpu.VMEM((chunks, half, ch), F32),
            pltpu.VMEM((chunks, half, ch), F32),
            pltpu.VMEM((peers, chunks, half, ch), F32),
            pltpu.VMEM((planes, cells, ch), BF16),
            pltpu.VMEM((planes, cells, ch), BF16),
            dma((4,)), dma((4,)), dma((2, 2)), dma((2, 2)),
            dma((chunks,)), dma((chunks,)), dma((chunks,)), dma((chunks,)), dma((chunks,)),
            dma((peers, chunks)), dma((peers, chunks)),
            dma((chunks,)), dma((chunks,)), dma((chunks,)), dma((chunks,)), dma((chunks,)),
            dma((3,)),
        ],
        compiler_params=pltpu.CompilerParams(
            collective_id=0, has_side_effects=True, vmem_limit_bytes=(24 + peers) * 1024 * 1024),
        cost_estimate=pl.CostEstimate(flops=flops, bytes_accessed=10_000_000, transcendentals=0),
    )(
        volume.reshape(planes, cells, ch),
        kernel,
        grad_out.reshape(planes, cells, ch),
    )
    activation = outs[0].reshape(volume.shape)
    input_grad = outs[1].reshape(volume.shape)
    return activation, input_grad, outs[2].reshape(3, 3, 3, ch, ch)


def solution(mesh):
    n = mesh.shape["slab"]
    chips = n // 2
    cols = 1
    while cols * cols * 4 <= chips:
        cols *= 2
    line = chips // cols
    return jax.shard_map(
        functools.partial(body, n, line, cols),
        mesh=mesh,
        in_specs=(
            P(("groups", "slab"), None, None, None),
            P(),
            P(("groups", "slab"), None, None, None),
        ),
        out_specs=(
            P(("groups", "slab"), None, None, None),
            P(("groups", "slab"), None, None, None),
            P("groups", None, None, None, None),
        ),
        check_vma=False,
    )
```

```python
import functools

import jax
import jax.numpy as jnp
import numpy as np
from jax import lax
from jax.experimental import pallas as pl
from jax.experimental.pallas import tpu as pltpu
from jax.sharding import PartitionSpec as P

MESH = pl.DeviceIdType.MESH
F32 = jnp.float32
BF16 = jnp.bfloat16


def layer_kernel(
    n, line, cols, height, breadth, ch, tile, factor,
    vol, ker, grd,
    act_out, ing_out, dw_out,
    vp, gp, wf, wk, wb, xt, gs, acc, fin, r_sib, r_lo, r_hi, r_y, act, ing,
    s_in, s_w, s_hs, s_hr, s_sib, r_sibs, s_line, r_los, r_his, s_y, r_ys,
    s_up, s_dn, s_fs, r_fin, r_fsib, s_out,
):
    cells = height * breadth
    half = ch // 2
    taps = 9
    me = lax.axis_index("slab")
    core = lax.rem(me, 2)
    chip = me // 2
    z = chip // cols
    y = lax.rem(chip, cols)
    sib = me + 1 - 2 * core
    zlo = me - 2 * cols
    zhi = me + 2 * cols
    has_lo, has_hi = z > 0, z < line - 1
    has_before, has_after = me > 0, me < n - 1

    def peer(k):
        return (z * cols + lax.rem(y + k, cols)) * 2 + core

    inner = pl.ds(breadth, cells)
    loads = []
    for p in range(2):
        loads.append(pltpu.make_async_copy(vol.at[p], vp.at[p + 1, inner], s_in.at[p]))
    for p in range(2):
        loads.append(pltpu.make_async_copy(grd.at[p], gp.at[p + 1, inner], s_in.at[p + 2]))
    for copy in loads:
        copy.start()
    wloads = []
    for c in range(3):
        wloads.append(pltpu.make_async_copy(
            ker.at[:, :, c], wf.at[:, :, :, pl.ds(c * ch, ch)], s_w.at[c]))
    wloads.append(pltpu.make_async_copy(ker, wk, s_w.at[3]))
    for copy in wloads:
        copy.start()

    barrier = pltpu.get_barrier_semaphore()

    def greet(dev):
        pl.semaphore_signal(barrier, inc=1, device_id={"slab": dev}, device_id_type=MESH)

    for k in range(1, cols):
        greet(peer(k))
    for cond, dev in ((has_before, me - 1), (has_after, me + 1), (has_lo, zlo), (has_hi, zhi)):
        @pl.when(cond)
        def _(dev=dev):
            greet(dev)
    partners = cols - 1
    for cond in (has_before, has_after, has_lo, has_hi):
        partners = partners + cond.astype(jnp.int32)
    pl.semaphore_wait(barrier, partners)

    def remote(src, dst, ssem, rsem, dev):
        return pltpu.make_async_remote_copy(
            src_ref=src, dst_ref=dst, send_sem=ssem, recv_sem=rsem,
            device_id={"slab": dev}, device_id_type=MESH)

    off_chip = jnp.where(core == 0, has_before, has_after)
    off_dev = me - 1 + 2 * core
    inside = 1 - core
    slot_sib, slot_off = 3 * inside, 3 * core

    def halo_sibling(which, src, dst):
        return remote(src.at[inside], dst.at[3 * core, inner], s_hs.at[which, 0], s_hr.at[which, 0], sib)

    def halo_off(which, src, dst):
        return remote(src.at[core], dst.at[3 * inside, inner], s_hs.at[which, 1], s_hr.at[which, 1], off_dev)

    def await_sibling(which, src, dst):
        remote(src.at[inside], dst.at[slot_sib, inner], s_hs.at[which, 0], s_hr.at[which, 0], sib).wait_recv()

    def await_off(which, src, dst):
        @pl.when(off_chip)
        def _():
            remote(src.at[core], dst.at[slot_off, inner], s_hs.at[which, 1], s_hr.at[which, 1], off_dev).wait_recv()

    @pl.when(off_chip)
    def _():
        halo_off(0, vol, vp).start()

    halo_sibling(0, vol, vp).start()
    halo_sibling(1, grd, gp).start()

    @pl.when(off_chip)
    def _():
        halo_off(1, grd, gp).start()

    edge = jnp.zeros((breadth, ch), BF16)
    for ref in (vp, gp):
        for p in range(4):
            ref[p, pl.ds(0, breadth), :] = edge
            ref[p, pl.ds(breadth + cells, breadth), :] = edge
    for c in range(3):
        for d in range(2):
            gs[c, d, pl.ds(0, breadth), :] = edge
            gs[c, d, pl.ds(breadth + cells, breadth), :] = edge
    for cond, p in ((me == 0, 0), (me == n - 1, 3)):
        @pl.when(cond)
        def _(p=p):
            vp[p, inner, :] = jnp.zeros((cells, ch), BF16)
            gp[p, inner, :] = jnp.zeros((cells, ch), BF16)

    rows = tile * breadth
    tiles = height // tile
    column = lax.rem(lax.broadcasted_iota(jnp.int32, (rows, ch), 0), breadth)

    def before_of(v):
        return jnp.where(column == 0, 0.0, pltpu.roll(v, 1, 0))

    def after_of(v):
        return jnp.where(column == breadth - 1, 0.0, pltpu.roll(v, rows - 1, 0))

    for copy in loads:
        copy.wait()

    def shift_tile(k, carry):
        at = pl.ds(pl.multiple_of(breadth + k * rows, 16), rows)
        for d in range(2):
            plane = gp[d + 1, at, :]
            wide = plane.astype(F32)
            gs[0, d, at, :] = after_of(wide).astype(BF16)
            gs[1, d, at, :] = plane
            gs[2, d, at, :] = before_of(wide).astype(BF16)
        return carry

    lax.fori_loop(0, tiles, shift_tile, 0)

    def transpose_planes(pairs):
        def one(j, carry):
            at = pl.ds(pl.multiple_of(breadth + j * ch, 16), ch)
            to = pl.ds(pl.multiple_of(j * ch, ch), ch)
            for p, row in pairs:
                xt[pl.ds(row * ch, ch), to] = vp[p, at, :].T
            return carry
        lax.fori_loop(0, cells // ch, one, 0)

    def grads(t, d):
        b, c = t // 3, lax.rem(t, 3)
        return gs[c, d, pl.ds(pl.multiple_of((2 - b) * breadth, 16), cells), :]

    await_sibling(0, vol, vp)
    transpose_planes(((1, 0), (2, 1), (slot_sib, 2)))

    def own_part(t, carry):
        rhs = jnp.concatenate([grads(t, 0), grads(t, 1)], axis=1)
        full = jnp.dot(xt[pl.ds(0, 3 * ch), :], rhs, preferred_element_type=F32)
        beside = full[2 * ch:]
        acc[0, t] = full[:ch, ch:] + jnp.where(core == 1, beside[:, :ch], 0.0)
        acc[1, t] = full[:ch, :ch] + full[ch:2 * ch, ch:]
        acc[2, t] = full[ch:2 * ch, :ch] + jnp.where(core == 0, beside[:, ch:], 0.0)
        return carry

    lax.fori_loop(0, taps, own_part, 0)

    def conv_tile(planes, weights, out, d, k, backward):
        start = k * rows
        bands = []
        for a in range(3):
            for b in range(3):
                at = pl.ds(pl.multiple_of(start + b * breadth, 16), rows)
                bands.append(planes[d + a, at, :])
        lhs = jnp.concatenate(bands, axis=1)
        if backward:
            rhs = weights[...]
        else:
            rhs = jnp.concatenate([weights[a, b] for a in range(3) for b in range(3)], axis=0)
        sums = jnp.dot(lhs, rhs, preferred_element_type=F32)
        first, last = sums[:, :ch], sums[:, 2 * ch:]
        total = sums[:, ch:2 * ch] + before_of(first) + after_of(last)
        out[d, pl.ds(pl.multiple_of(start, 16), rows), :] = total.astype(BF16)

    for copy in wloads:
        copy.wait()
    for a in range(3):
        for b in range(3):
            for c in range(3):
                wb[pl.ds((3 * a + b) * ch, ch), pl.ds(c * ch, ch)] = wk[2 - a, 2 - b, 2 - c].T

    def inside_act(k, carry):
        conv_tile(vp, wf, act, inside, k, False)
        return carry

    def inside_ing(k, carry):
        conv_tile(gp, wb, ing, inside, k, True)
        return carry

    lax.fori_loop(0, tiles, inside_act, 0)
    await_sibling(1, grd, gp)
    lax.fori_loop(0, tiles, inside_ing, 0)

    await_off(0, vol, vp)

    transpose_planes(((slot_off, 3),))

    mine = pl.ds(pl.multiple_of(core * half, half), half)
    other = pl.ds(pl.multiple_of((1 - core) * half, half), half)

    def root(j):
        return (line - 1) // 2 + lax.rem(j, 2) * (line // 2 - (line - 1) // 2)

    def to_sibling(j):
        return remote(acc.at[:, j, other], r_sib.at[j], s_sib.at[j], r_sibs.at[j], sib)

    def line_up(j):
        return remote(acc.at[:, j, mine], r_lo.at[j], s_line.at[j], r_los.at[j], zhi)

    def line_down(j):
        return remote(acc.at[:, j, mine], r_hi.at[j], s_line.at[j], r_his.at[j], zlo)

    def across(j, k):
        return remote(acc.at[:, j, mine], r_y.at[k - 1, j], s_y.at[k - 1, j], r_ys.at[k - 1, j], peer(k))

    def final_up(j):
        return remote(fin.at[:, j, mine], fin.at[:, j, mine], s_up.at[j], r_fin.at[j], zhi)

    def final_down(j):
        return remote(fin.at[:, j, mine], fin.at[:, j, mine], s_dn.at[j], r_fin.at[j], zlo)

    def final_sibling(j):
        return remote(fin.at[:, j, mine], fin.at[:, j, mine], s_fs.at[j], r_fsib.at[j], sib)

    def stage_send(j):
        part = jnp.dot(xt[pl.ds(3 * ch, ch), :], grads(j, core), preferred_element_type=F32)
        acc[2 * core, j] = acc[2 * core, j] + part
        to_sibling(j).start()

    def stage_sibling(j):
        to_sibling(j).wait_recv()
        acc[:, j, mine, :] = acc[:, j, mine, :] + r_sib[j]

        @pl.when(jnp.logical_and(z == 0, root(j) != 0))
        def _():
            line_up(j).start()

        @pl.when(jnp.logical_and(z == line - 1, root(j) != line - 1))
        def _():
            line_down(j).start()

    def stage_line(j):
        @pl.when(jnp.logical_and(z > 0, z < root(j)))
        def _():
            line_up(j).wait_recv()
            acc[:, j, mine, :] = acc[:, j, mine, :] + r_lo[j]
            line_up(j).start()

        @pl.when(jnp.logical_and(z < line - 1, z > root(j)))
        def _():
            line_down(j).wait_recv()
            acc[:, j, mine, :] = acc[:, j, mine, :] + r_hi[j]
            line_down(j).start()

    def stage_root(j):
        @pl.when(z == root(j))
        def _():
            @pl.when(has_lo)
            def _():
                line_up(j).wait_recv()
                acc[:, j, mine, :] = acc[:, j, mine, :] + r_lo[j]

            @pl.when(has_hi)
            def _():
                line_down(j).wait_recv()
                acc[:, j, mine, :] = acc[:, j, mine, :] + r_hi[j]

            for k in range(1, cols):
                across(j, k).start()

    def stage_across(j):
        @pl.when(z == root(j))
        def _():
            for k in range(1, cols):
                across(j, k).wait_recv()
            if cols <= 2:
                total = acc[:, j, mine, :]
                for k in range(1, cols):
                    total = total + r_y[k - 1, j]
            else:
                total = jnp.zeros((3, half, ch), F32)
                for i in range(cols):
                    term = acc[:, j, mine, :]
                    for k in range(1, cols):
                        term = jnp.where(lax.rem(y + cols - k, cols) == i, r_y[k - 1, j], term)
                    total = total + term
            fin[:, j, mine, :] = total * factor

            @pl.when(has_lo)
            def _():
                final_down(j).start()

            @pl.when(has_hi)
            def _():
                final_up(j).start()

            final_sibling(j).start()

    def stage_spread(j):
        @pl.when(z < root(j))
        def _():
            final_down(j).wait_recv()

            @pl.when(has_lo)
            def _():
                final_down(j).start()

            final_sibling(j).start()

        @pl.when(z > root(j))
        def _():
            final_up(j).wait_recv()

            @pl.when(has_hi)
            def _():
                final_up(j).start()

            final_sibling(j).start()

    def during(j, stage):
        @pl.when(jnp.logical_and(j >= 0, j < taps))
        def _():
            stage(j)

    lags = (
        (1, stage_sibling), (3, stage_line), (5, stage_root),
        (7, stage_across), (10, stage_spread),
    )
    steps = max(taps + 10, 2 * tiles)

    def step(s, carry):
        during(s, stage_send)

        @pl.when(s < tiles)
        def _():
            conv_tile(vp, wf, act, core, s, False)

        @pl.when(s == tiles)
        def _():
            await_off(1, grd, gp)

        @pl.when(jnp.logical_and(s >= tiles, s < 2 * tiles))
        def _():
            conv_tile(gp, wb, ing, core, s - tiles, True)

        for lag, stage in lags:
            during(s - lag, stage)
        return carry

    lax.fori_loop(0, steps, step, 0)

    act_copy = pltpu.make_async_copy(act, act_out, s_out.at[0])
    ing_copy = pltpu.make_async_copy(ing, ing_out, s_out.at[1])
    dw_copy = pltpu.make_async_copy(fin, dw_out, s_out.at[2])
    act_copy.start()
    ing_copy.start()

    def finish(j, carry):
        to_sibling(j).wait_send()
        final_sibling(j).wait_send()

        @pl.when(z != root(j))
        def _():
            line_up(j).wait_send()

        @pl.when(z == root(j))
        def _():
            for k in range(1, cols):
                across(j, k).wait_send()

        @pl.when(jnp.logical_and(has_lo, z <= root(j)))
        def _():
            final_down(j).wait_send()

        @pl.when(jnp.logical_and(has_hi, z >= root(j)))
        def _():
            final_up(j).wait_send()

        final_sibling(j).wait_recv()
        return carry

    lax.fori_loop(0, taps, finish, 0)
    dw_copy.start()

    for which, src, dst in ((0, vol, vp), (1, grd, gp)):
        halo_sibling(which, src, dst).wait_send()

        @pl.when(off_chip)
        def _(which=which, src=src, dst=dst):
            halo_off(which, src, dst).wait_send()

    act_copy.wait()
    ing_copy.wait()
    dw_copy.wait()


def body(n, line, cols, volume, kernel, grad_out):
    planes, height, breadth, ch = volume.shape
    cells = height * breadth
    half = ch // 2
    taps = 9
    tile = 8
    factor = float(np.float32(1.0) / np.sqrt(np.float32(n * planes * cells)))
    dma = pltpu.SemaphoreType.DMA
    peers = max(cols - 1, 1)
    flops = 3 * 2 * 27 * planes * cells * ch * ch
    outs = pl.pallas_call(
        functools.partial(layer_kernel, n, line, cols, height, breadth, ch, tile, factor),
        out_shape=(
            jax.ShapeDtypeStruct((planes, cells, ch), BF16),
            jax.ShapeDtypeStruct((planes, cells, ch), BF16),
            jax.ShapeDtypeStruct((3, taps, ch, ch), F32),
        ),
        in_specs=[pl.BlockSpec(memory_space=pl.ANY)] * 3,
        out_specs=[pl.BlockSpec(memory_space=pl.ANY)] * 3,
        scratch_shapes=[
            pltpu.VMEM((4, cells + 2 * breadth, ch), BF16),
            pltpu.VMEM((4, cells + 2 * breadth, ch), BF16),
            pltpu.VMEM((3, 3, ch, 3 * ch), BF16),
            pltpu.VMEM((3, 3, 3, ch, ch), BF16),
            pltpu.VMEM((9 * ch, 3 * ch), BF16),
            pltpu.VMEM((4 * ch, cells), BF16),
            pltpu.VMEM((3, 2, cells + 2 * breadth, ch), BF16),
            pltpu.VMEM((3, taps, ch, ch), F32),
            pltpu.VMEM((3, taps, ch, ch), F32),
            pltpu.VMEM((taps, 3, half, ch), F32),
            pltpu.VMEM((taps, 3, half, ch), F32),
            pltpu.VMEM((taps, 3, half, ch), F32),
            pltpu.VMEM((peers, taps, 3, half, ch), F32),
            pltpu.VMEM((planes, cells, ch), BF16),
            pltpu.VMEM((planes, cells, ch), BF16),
            dma((4,)), dma((4,)), dma((2, 2)), dma((2, 2)),
            dma((taps,)), dma((taps,)), dma((taps,)), dma((taps,)), dma((taps,)),
            dma((peers, taps)), dma((peers, taps)),
            dma((taps,)), dma((taps,)), dma((taps,)), dma((taps,)), dma((taps,)),
            dma((3,)),
        ],
        compiler_params=pltpu.CompilerParams(
            collective_id=0, has_side_effects=True, vmem_limit_bytes=56 * 1024 * 1024),
        cost_estimate=pl.CostEstimate(flops=flops, bytes_accessed=10_000_000, transcendentals=0),
    )(
        volume.reshape(planes, cells, ch),
        kernel,
        grad_out.reshape(planes, cells, ch),
    )
    activation = outs[0].reshape(volume.shape)
    input_grad = outs[1].reshape(volume.shape)
    return activation, input_grad, outs[2].reshape(3, 3, 3, ch, ch)


def solution(mesh):
    n = mesh.shape["slab"]
    chips = n // 2
    cols = 1
    while cols * cols * 4 <= chips:
        cols *= 2
    line = chips // cols
    return jax.shard_map(
        functools.partial(body, n, line, cols),
        mesh=mesh,
        in_specs=(
            P(("groups", "slab"), None, None, None),
            P(),
            P(("groups", "slab"), None, None, None),
        ),
        out_specs=(
            P(("groups", "slab"), None, None, None),
            P(("groups", "slab"), None, None, None),
            P("groups", None, None, None, None),
        ),
        check_vma=False,
    )
```
